32 devices in a mesh: dp: 8 (over z, core), blk: 4 (over y, x).
Axes of the slice: x: 2, y: 2, z: 4, core: 2. Of those that a mesh axis runs over, the one named last changes fastest.
Arguments:
- frames: bfloat16 [32, 1280, 256], P('dp', 'blk'), may hold values from -6 to 6
- weight: bfloat16 [1280, 11520], P('blk'), may hold values from -0.0546875 to 0.0546875
- bias: float32 [1280], P('blk'), may hold values from -3 to 3
- cotangent: bfloat16 [32, 1280, 256], P('dp', 'blk'), may hold values from -6 to 6
Outputs:
- response: bfloat16 [32, 1280, 256], P('dp', 'blk')
- frame_grad: bfloat16 [32, 1280, 256], P('dp', 'blk')
- weight_grad: float32 [1280, 11520], P(('blk', 'dp'))
The draws below stay inside these ranges and needn't reach their ends.
All inputs are finite; a program needn't handle non-finite values.
Results may differ from the reference program's by a relative error of at most 0.001.
Values may be sent and summed in bfloat16 or wider, within the bound.
No kernel may reach another device: no remote copies, remote signals or barrier semaphores. Data moves between devices by JAX's collectives and lax.ppermute only.
A program may use at most 128 MiB of HBM per device.

```python
import jax
import jax.numpy as jnp
from jax import lax

C = 1280
H = 16
WD = 16
FRAMES = 32


def strengthened(result, stream_key, source, target, parts, factor):
    def block_of(axis_at):
        return (jnp.arange(result.shape[axis_at]) // (result.shape[axis_at] // parts)).reshape((-1,) + (1,) * (result.ndim - 1 - axis_at))

    one_side = jax.random.permutation(stream_key, parts)[block_of(target)]
    other_side = (block_of(target) + parts // 2) % parts
    return jnp.where((block_of(source) == one_side) | (block_of(source) == other_side), factor * result, result)


def levels(key, shape, shards, least, largest):
    factor_of, own = 1.0, jax.random.fold_in(key, 6)
    for dim, parts in shards:
        draws = jnp.exp(jax.random.uniform(jax.random.fold_in(own, dim), (parts,), jnp.float32, least / len(shards), largest / len(shards)))
        factor_of = factor_of * jnp.repeat(draws, shape[dim] // parts).reshape([-1 if axis == dim else 1 for axis in range(len(shape))])
    return factor_of


def bell_draw(own_key, shape, width, bound, cuts=(), held_as=jnp.bfloat16):
    loudness = levels(own_key, shape, cuts, -0.22, 0.18) if cuts else 1.0
    values = jax.random.normal(own_key, shape, jnp.float32) * width * loudness
    return jnp.minimum(jnp.maximum(values, -bound), bound).astype(held_as)


def bell_draw_with(rng, extent, width, limit, cuts, heavy, held_as=jnp.bfloat16):
    result = width * jax.random.normal(rng, extent, jnp.float32)
    if cuts:
        result = result * levels(rng, extent, cuts, -0.22, 0.18)
    return jnp.clip(strengthened(result, jax.random.fold_in(rng, 3), *heavy), -limit, limit).astype(held_as)


def setup_inputs(seed: int = 0) -> dict:
    seeds = jax.random.split(jax.random.key(seed), 5)
    frames = bell_draw_with(seeds[0], (FRAMES, C, H * WD), 1.0, 6.0, ((0, 8), (1, 4)), (0, 1, 8, 2.0))
    weight = bell_draw(seeds[1], (C, 9 * C), (9 * C) ** -0.5, 0.0546875, ((0, 4),))
    bias = bell_draw(seeds[2], (C,), 0.5, 3.0, ((0, 4),), jnp.float32)
    cotangent = bell_draw(seeds[3], (FRAMES, C, H * WD), 1.0, 6.0, ((0, 8), (1, 4)))
    return {"frames": frames, "weight": weight, "bias": bias, "cotangent": cotangent}


def reference(frames, weight, bias, cotangent):
    nf, chans, cells = frames.shape
    rows = cells // WD
    cols = WD
    maps = jnp.transpose(frames.reshape(nf, chans, rows, cols), (0, 2, 3, 1))
    cot_maps = jnp.transpose(cotangent.reshape(nf, chans, rows, cols), (0, 2, 3, 1))
    padded = jnp.pad(maps, ((0, 0), (1, 1), (1, 1), (0, 0)))
    cot_padded = jnp.pad(cot_maps, ((0, 0), (1, 1), (1, 1), (0, 0)))
    cot_flat = cot_maps.reshape(-1, chans)
    total = jnp.zeros((nf * rows * cols, chans), jnp.float32)
    back = jnp.zeros((nf * rows * cols, chans), jnp.float32)
    grads = []
    for tap in range(9):
        ky, kx = divmod(tap, 3)
        w_tap = weight[:, tap * chans:(tap + 1) * chans]
        piece = padded[:, ky:ky + rows, kx:kx + cols, :].reshape(-1, chans)
        total = total + jnp.dot(piece, w_tap.T, preferred_element_type=jnp.float32)
        grads.append(lax.dot_general(cot_flat, piece, (((0,), (0,)), ((), ())), preferred_element_type=jnp.float32))
        cpiece = cot_padded[:, 2 - ky:2 - ky + rows, 2 - kx:2 - kx + cols, :].reshape(-1, chans)
        back = back + jnp.dot(cpiece, w_tap, preferred_element_type=jnp.float32)
    total = total + bias[None, :]
    response = jnp.transpose(total.reshape(nf, cells, chans), (0, 2, 1)).astype(jnp.bfloat16)
    frame_grad = jnp.transpose(back.reshape(nf, cells, chans), (0, 2, 1)).astype(jnp.bfloat16)
    weight_grad = jnp.concatenate(grads, axis=1)
    return response, frame_grad, weight_grad
```

```python
import functools

import jax
import jax.numpy as jnp
from jax import lax
from jax.experimental import pallas as pl
from jax.experimental.pallas import tpu as pltpu
from jax.sharding import PartitionSpec as P

WD = 16
TAPS = 9
F32, BF16 = jnp.float32, jnp.bfloat16
NT = (((1,), (1,)), ((), ()))
TN = (((0,), (0,)), ((), ()))
VMEM = pl.BlockSpec(memory_space=pltpu.VMEM)
ANY = pl.BlockSpec(memory_space=pl.ANY)
SPAN = 125.0


def shift_cells(maps, step_row, step_col):
    cells = maps.shape[-1]
    margin = WD + 1
    widths = [(0, 0)] * (maps.ndim - 1) + [(margin, margin)]
    flat = jnp.pad(maps, widths)
    begin = margin + step_row * WD + step_col
    moved = lax.slice_in_dim(flat, begin, begin + cells, axis=maps.ndim - 1)
    column = jnp.arange(cells, dtype=jnp.int32) % WD + step_col
    keeper = ((column >= 0) & (column < WD)).astype(maps.dtype)
    return moved * keeper


def general_body(frames, weight, bias, cotangent):
    nframe = frames.shape[0]
    local_ch = frames.shape[1]
    cells = frames.shape[2]
    whole = lax.all_gather(frames, "blk", axis=1, tiled=True)
    all_ch = whole.shape[1]
    total = jnp.zeros((nframe, local_ch, cells), F32)
    grads = []
    for tap in range(TAPS):
        ky, kx = divmod(tap, 3)
        piece = shift_cells(whole, ky - 1, kx - 1)
        w_tap = weight[:, tap * all_ch : (tap + 1) * all_ch]
        total = total + jnp.einsum("oi,fic->foc", w_tap, piece, preferred_element_type=F32)
        grads.append(
            lax.dot_general(cotangent, piece, (((0, 2), (0, 2)), ((), ())), preferred_element_type=F32)
        )
    response = (total + bias[None, :, None]).astype(BF16)
    local_grad = jnp.concatenate(grads, axis=1)
    weight_grad = lax.psum_scatter(local_grad, "dp", scatter_dimension=0, tiled=True)
    cot_moved = [shift_cells(cotangent, 1 - tap // 3, 1 - tap % 3) for tap in range(TAPS)]
    accum = jnp.zeros((all_ch, nframe, cells), F32)
    for tap in range(TAPS):
        w_cols = lax.slice_in_dim(weight, tap * all_ch, (tap + 1) * all_ch, axis=1)
        accum = accum + jnp.einsum("oi,foc->ifc", w_cols, cot_moved[tap], preferred_element_type=F32)
    shares = lax.psum_scatter(accum, "blk", scatter_dimension=0, tiled=True)
    frame_grad = jnp.transpose(shares, (1, 0, 2)).astype(BF16)
    return (response, frame_grad, weight_grad)


def scale_of(largest):
    return (jnp.maximum(largest, 1e-30) * 1.01).astype(BF16).astype(F32)


def encode(x, s):
    y = jnp.exp2(jnp.abs(x) * (2 * SPAN / s) - SPAN)
    return jnp.where(x < 0, -y, y)


def decode(code, s):
    y = code.astype(F32)
    v = (jnp.log2(jnp.abs(y)) + SPAN) * (s * (0.5 / SPAN))
    return jnp.where(y < 0, -v, v)


def cell_masks(rows, cells):
    lane = lax.broadcasted_iota(jnp.int32, (rows, cells), 1)
    return lane // WD, lane % WD


def moved(x, step, row, col, ky, kx):
    cells = x.shape[1]
    dy, dx = step * (ky - 1), step * (kx - 1)
    off = (dy * WD + dx) % cells
    out = pltpu.roll(x, off, 1) if off else x
    ok = None
    if dy:
        ok = (row >= dy) if dy > 0 else (row < cells // WD + dy)
    if dx:
        okx = (col >= dx) if dx > 0 else (col < WD + dx)
        ok = okx if ok is None else ok & okx
    return out if ok is None else jnp.where(ok, out, 0.0)


def put_rows_coded(out_ref, lead, values, width):
    rows, padded = values.shape
    s = scale_of(jnp.max(jnp.abs(values), axis=1, keepdims=True))
    codes = encode(values, s)
    last = padded - 128
    lane = lax.broadcasted_iota(jnp.int32, (rows, 128), 1) + last
    out_ref[lead + (slice(None), slice(0, last))] = codes[:, :last].astype(BF16)
    tail = jnp.where(lane < width, codes[:, last:], s)
    out_ref[lead + (slice(None), slice(last, padded))] = tail.astype(BF16)


def take_rows_coded(code, width):
    s = code[:, width : width + 1].astype(F32)
    return decode(code, s)


def weight_sums(first, width, cs_ref, xs_ref, chunks, f_ref, send_ref, keep_ref, wait):
    pieces = f_ref.shape[0]
    ch = xs_ref.shape[0] // pieces
    rows = f_ref.shape[1]
    half = rows // 2
    pad = f_ref.shape[2] - width
    for p in range(pieces):
        f_ref[p, :, width:] = jnp.zeros((rows, pad), F32)
    per = TAPS // chunks
    for chunk in range(chunks):
        if wait is not None:
            wait(chunk)
        got = lax.dot_general(
            cs_ref[chunk * per * rows : (chunk + 1) * per * rows, :], xs_ref[...], NT, preferred_element_type=F32
        )
        for k in range(per):
            t = chunk * per + k
            for p in range(pieces):
                f_ref[p, :, t * ch : (t + 1) * ch] = got[k * rows : (k + 1) * rows, p * ch : (p + 1) * ch]
    for p in range(pieces):
        keep_ref[p] = f_ref[p, :half, :]
        put_rows_coded(send_ref, (p,), f_ref[p, half:, :], width)


def first_weight_kernel(width, cot_ref, cot2_ref, x_ref, x2_ref, send_ref, keep_ref, cs_out, cs_ref, xs_ref, f_ref, sem):
    nf, ch, cells = cot_ref.shape
    rows = f_ref.shape[1]
    block = rows // 4
    me = lax.axis_index("dp")
    z, core = me // 2, me % 2
    a = lax.broadcasted_iota(jnp.int32, (rows, ch), 0)
    o = lax.broadcasted_iota(jnp.int32, (rows, ch), 1)
    j = (a >= block).astype(jnp.int32) + (a >= 2 * block).astype(jnp.int32) + (a >= 3 * block).astype(jnp.int32)
    layer = jnp.where(j == 0, z, jnp.where(j == 1, z ^ 2, jnp.where(j == 2, z ^ 1, z ^ 3)))
    want = (2 * layer + core) * block + a - j * block
    pick = (o == want).astype(F32).astype(BF16)
    row, col = cell_masks(rows, cells)
    for f in range(2 * nf):
        src = cot_ref if f < nf else cot2_ref
        chosen = jnp.dot(pick, src[f % nf], preferred_element_type=F32)
        for t in range(TAPS):
            ky, kx = divmod(t, 3)
            cs_ref[t * rows : (t + 1) * rows, f * cells : (f + 1) * cells] = moved(
                chosen, 1, row, col, ky, kx
            ).astype(BF16)
        xsrc = x_ref if f < nf else x2_ref
        xs_ref[:, f * cells : (f + 1) * cells] = xsrc[f % nf]
    copy = pltpu.make_async_copy(cs_ref, cs_out, sem)
    copy.start()
    weight_sums(True, width, cs_ref, xs_ref, 3, f_ref, send_ref, keep_ref, None)
    copy.wait()


def later_weight_kernel(width, pieces, cs_hbm, *refs):
    xs = refs[: 2 * pieces]
    send_ref, keep_ref, cs_ref, xs_ref, f_ref, sem = refs[2 * pieces :]
    chunks = 3
    span = cs_ref.shape[0] // chunks
    copies = [
        pltpu.make_async_copy(
            cs_hbm.at[pl.ds(k * span, span)], cs_ref.at[pl.ds(k * span, span)], sem.at[k]
        )
        for k in range(chunks)
    ]
    for c in copies:
        c.start()
    nf, ch, cells = xs[0].shape
    for p in range(pieces):
        for f in range(2 * nf):
            src = xs[2 * p + f // nf]
            xs_ref[p * ch : (p + 1) * ch, f * cells : (f + 1) * cells] = src[f % nf]
    weight_sums(False, width, cs_ref, xs_ref, chunks, f_ref, send_ref, keep_ref, lambda k: copies[k].wait())


def second_weight_kernel(width, keep_ref, recv_ref, send_ref, keep2_ref):
    pieces, rows, padded = keep_ref.shape
    half = rows // 2
    for p in range(pieces):
        total = keep_ref[p] + take_rows_coded(recv_ref[p], width)
        keep2_ref[p] = total[:half]
        lane = lax.broadcasted_iota(jnp.int32, (half, padded), 1)
        far = jnp.where(lane < width, total[half:], 0.0)
        s = scale_of(jnp.max(jnp.abs(far), axis=1, keepdims=True))
        codes = jnp.where(lane < width, encode(far, s), s)
        if pieces == 1:
            left = send_ref.shape[1]
            fill = jnp.broadcast_to(s, (half, 2 * left - padded))
            right = jnp.concatenate([codes[:, left:], fill], axis=1)
            send_ref[...] = jnp.concatenate([codes[:, :left], right], axis=0).astype(BF16)
        else:
            f = codes
            if p == 0:
                held = f
            else:
                send_ref[...] = jnp.concatenate([held, f], axis=0).astype(BF16)


def last_weight_kernel(width, ka, ra, kb, rb, kc, rc, out_ref, acc):
    blk = lax.axis_index("blk")
    half = ka.shape[1]
    padded = ka.shape[2]
    ch = width // TAPS
    pieces = []
    for k, r in ((ka, ra), (kb, rb), (kc, rc)):
        if k.shape[0] == 1:
            left = r.shape[1]
            code = r[...].astype(F32)
            code = jnp.concatenate([code[:half], code[half:, : padded - left]], axis=1)
            pieces.append(k[0] + take_rows_coded(code, width))
        else:
            code = r[...].astype(F32)
            for p in range(2):
                pieces.append(k[p] + take_rows_coded(code[p * half : (p + 1) * half], width))
    for jj, v in enumerate(pieces):
        acc[blk ^ jj] = v
    nb = len(pieces)
    for q in range(nb):
        for t in range(TAPS):
            at = (t * nb + q) * ch
            out_ref[:, at : at + ch] = acc[q, :, t * ch : (t + 1) * ch]


def put_columns_coded(send_ref, lead, left, right):
    ch, cells = left.shape
    scales = []
    for k, v in enumerate((left, right)):
        s = scale_of(jnp.max(jnp.abs(v), axis=0, keepdims=True))
        send_ref[lead + (slice(k * ch, (k + 1) * ch),)] = encode(v, s).astype(BF16)
        scales.append(jnp.broadcast_to(s, (8, cells)))
    send_ref[lead + (slice(2 * ch, 2 * ch + 16),)] = jnp.concatenate(scales, axis=0).astype(BF16)


def take_columns_coded(ref, lead, ch):
    scales = ref[lead + (slice(2 * ch, 2 * ch + 16),)].astype(F32)
    return [
        decode(ref[lead + (slice(k * ch, (k + 1) * ch),)], scales[8 * k : 8 * k + 1]) for k in range(2)
    ]


def load_taps(w_hbm, w_ref, sem, rows, all_ch):
    copies = [
        pltpu.make_async_copy(
            w_hbm.at[:, pl.ds(t * all_ch, all_ch)], w_ref.at[pl.ds(t * rows, rows)], sem.at[t]
        )
        for t in range(TAPS)
    ]
    for c in copies:
        c.start()
    return copies


def frame_grad_kernel(mask, f0, w_hbm, cot_ref, send_ref, keep_ref, w_ref, cs_ref, out_ref, sem):
    nf, ch, cells = cot_ref.shape
    all_ch = w_ref.shape[1]
    copies = load_taps(w_hbm, w_ref, sem, ch, all_ch)
    row, col = cell_masks(ch, cells)
    for f in range(2):
        x = cot_ref[f0 + f].astype(F32)
        for t in range(TAPS):
            ky, kx = divmod(t, 3)
            cs_ref[t * ch : (t + 1) * ch, f * cells : (f + 1) * cells] = moved(x, 1, row, col, ky, kx).astype(BF16)
    for c in copies:
        c.wait()
    tile = 256
    for i0 in range(0, all_ch, tile):
        out_ref[i0 : i0 + tile, :] = lax.dot_general(
            w_ref[:, i0 : i0 + tile], cs_ref[...], TN, preferred_element_type=F32
        )
    blk = lax.axis_index("blk")

    def block(q, f):
        return out_ref[pl.ds(pl.multiple_of(q * ch, 16), ch), f * cells : (f + 1) * cells]

    for k, q in enumerate((blk ^ mask, blk ^ 3)):
        put_columns_coded(send_ref, (k,), block(q, 0), block(q, 1))
    for k, q in enumerate((blk, blk ^ (3 - mask))):
        for f in range(2):
            keep_ref[k, f * ch : (f + 1) * ch, :] = block(q, f)


def second_frame_kernel(kx, rx, ky, ry, sx, k2x, sy, k2y):
    ch = kx.shape[1] // 2
    for k, r, s, k2 in ((kx, rx, sx, k2x), (ky, ry, sy, k2y)):
        for b in range(2):
            got = take_columns_coded(r, (b,), ch)
            sums = [k[b, f * ch : (f + 1) * ch, :] + got[f] for f in range(2)]
            if b == 0:
                for f in range(2):
                    k2[f * ch : (f + 1) * ch, :] = sums[f]
            else:
                put_columns_coded(s, (), sums[0], sums[1])


def last_frame_kernel(kx, rx, ky, ry, out_ref):
    ch = out_ref.shape[1]
    for h, (k, r) in enumerate(((kx, rx), (ky, ry))):
        got = take_columns_coded(r, (), ch)
        for f in range(2):
            out_ref[2 * h + f] = (k[f * ch : (f + 1) * ch, :] + got[f]).astype(BF16)


def response_kernel(w_hbm, bias_ref, x0, x1, x2, x3, out_ref, w_ref, x_ref, y_ref, sem):
    _, ch, cells = x0.shape
    all_ch = w_ref.shape[1]
    blk = lax.axis_index("blk")

    @pl.when(pl.program_id(0) == 0)
    def _():
        for c in load_taps(w_hbm, w_ref, sem, ch, all_ch):
            c.wait()

    for jj, x in enumerate((x0, x1, x2, x3)):
        x_ref[pl.ds(pl.multiple_of((blk ^ jj) * ch, 16), ch), :] = x[0]
    y_ref[...] = jnp.dot(w_ref[...], x_ref[...], preferred_element_type=F32)
    row, col = cell_masks(ch, cells)
    total = jnp.broadcast_to(bias_ref[...], (ch, cells))
    for t in range(TAPS):
        ky, kx = divmod(t, 3)
        total = total + moved(y_ref[t * ch : (t + 1) * ch, :], -1, row, col, ky, kx)
    out_ref[0] = total.astype(BF16)


def params(mib=48):
    return pltpu.CompilerParams(vmem_limit_bytes=mib * 2**20)


def shape(dims, dtype):
    return jax.ShapeDtypeStruct(dims, dtype)


def swap_core(x):
    return lax.ppermute(x, "dp", [(d, d ^ 1) for d in range(8)])


def swap_layer(x, mask):
    return lax.ppermute(x, "dp", [(d, d ^ (2 * mask)) for d in range(8)])


def swap_block(x, mask):
    return lax.ppermute(x, "blk", [(d, d ^ mask) for d in range(4)])


def small_body(frames, weight, bias, cotangent):
    nf, ch, cells = frames.shape
    all_ch = 4 * ch
    rows = ch // 2
    half, quarter = rows // 2, rows // 4
    width = TAPS * ch
    padded = -(-(width + 1) // 128) * 128
    left = -(-(padded // 2) // 128) * 128
    deep = 2 * nf * cells

    def cost(flops, nbytes):
        return pl.CostEstimate(flops=flops, bytes_accessed=nbytes, transcendentals=0)

    work = 2 * nf * cells * ch * all_ch * TAPS

    cot2 = swap_core(cotangent)
    own2 = swap_core(frames)
    near_x = swap_block(frames, 1)
    near_y = swap_block(frames, 2)

    send_a, keep_a, cs = pl.pallas_call(
        functools.partial(first_weight_kernel, width),
        out_shape=(
            shape((1, half, padded), BF16),
            shape((1, half, padded), F32),
            shape((TAPS * rows, deep), BF16),
        ),
        in_specs=[VMEM] * 4,
        out_specs=(VMEM, VMEM, ANY),
        scratch_shapes=[
            pltpu.VMEM((TAPS * rows, deep), BF16),
            pltpu.VMEM((ch, deep), BF16),
            pltpu.VMEM((1, rows, padded), F32),
            pltpu.SemaphoreType.DMA,
        ],
        compiler_params=params(),
        cost_estimate=cost(work // 4, 16 * 2**20),
        name="weight_first",
    )(cotangent, cot2, frames, own2)
    recv_a = swap_layer(send_a, 1)

    def frame_part(mask, f0):
        return pl.pallas_call(
            functools.partial(frame_grad_kernel, mask, f0),
            out_shape=(
                shape((2, 2 * ch + 16, cells), BF16),
                shape((2, 2 * ch, cells), F32),
            ),
            in_specs=[ANY, VMEM],
            out_specs=(VMEM, VMEM),
            scratch_shapes=[
                pltpu.VMEM((TAPS * ch, all_ch), BF16),
                pltpu.VMEM((TAPS * ch, 2 * cells), BF16),
                pltpu.VMEM((all_ch, 2 * cells), F32),
                pltpu.SemaphoreType.DMA((TAPS,)),
            ],
            compiler_params=params(),
            cost_estimate=cost(work // 2, 16 * 2**20),
            name="frame_part",
        )(weight, cotangent)

    diag = swap_block(frames, 3)
    fsend_x, fkeep_x = frame_part(1, 0)

    def later(xs):
        n = len(xs) // 2
        return pl.pallas_call(
            functools.partial(later_weight_kernel, width, n),
            out_shape=(shape((n, half, padded), BF16), shape((n, half, padded), F32)),
            in_specs=[ANY] + [VMEM] * (2 * n),
            out_specs=(VMEM, VMEM),
            scratch_shapes=[
                pltpu.VMEM((TAPS * rows, deep), BF16),
                pltpu.VMEM((n * ch, deep), BF16),
                pltpu.VMEM((n, rows, padded), F32),
                pltpu.SemaphoreType.DMA((3,)),
            ],
            compiler_params=params(),
            cost_estimate=cost(work * n // 4, 16 * 2**20),
            name="weight_later",
        )(cs, *xs)

    def second(keep, recv):
        n = keep.shape[0]
        out = (2 * quarter, padded) if n == 2 else (2 * quarter, left)
        return pl.pallas_call(
            functools.partial(second_weight_kernel, width),
            out_shape=(shape(out, BF16), shape((n, quarter, padded), F32)),
            in_specs=[VMEM] * 2,
            out_specs=(VMEM, VMEM),
            compiler_params=params(),
            cost_estimate=cost(0, 4 * 2**20),
            name="weight_second",
        )(keep, recv)

    near_x2 = swap_core(near_x)
    near_y2 = swap_core(near_y)
    send_b, keep_b = later([near_x, near_x2, near_y, near_y2])
    recv_b = swap_layer(send_b, 1)
    send_a2, keep_a2 = second(keep_a, recv_a)
    recv_a2 = swap_layer(send_a2, 2)

    frecv_x = swap_block(fsend_x, 1)
    fsend_y, fkeep_y = frame_part(2, 2)
    frecv_y = swap_block(fsend_y, 2)

    diag2 = swap_core(diag)
    send_c, keep_c = later([diag, diag2])
    recv_c = swap_layer(send_c, 1)

    piece = pl.BlockSpec((1, ch, cells), lambda f: (f, 0, 0))
    response = pl.pallas_call(
        response_kernel,
        grid=(nf,),
        out_shape=shape((nf, ch, cells), BF16),
        in_specs=[ANY, pl.BlockSpec((ch, 1), lambda f: (0, 0))] + [piece] * 4,
        out_specs=piece,
        scratch_shapes=[
            pltpu.VMEM((TAPS * ch, all_ch), BF16),
            pltpu.VMEM((all_ch, cells), BF16),
            pltpu.VMEM((TAPS * ch, cells), F32),
            pltpu.SemaphoreType.DMA((TAPS,)),
        ],
        compiler_params=params(),
        cost_estimate=cost(work, 16 * 2**20),
        name="response",
    )(weight, bias.reshape(ch, 1), frames, near_x, near_y, diag)

    send_b2, keep_b2 = second(keep_b, recv_b)
    recv_b2 = swap_layer(send_b2, 2)
    fsum = pl.pallas_call(
        second_frame_kernel,
        out_shape=(
            shape((2 * ch + 16, cells), BF16),
            shape((2 * ch, cells), F32),
            shape((2 * ch + 16, cells), BF16),
            shape((2 * ch, cells), F32),
        ),
        in_specs=[VMEM] * 4,
        out_specs=(VMEM,) * 4,
        compiler_params=params(),
        cost_estimate=cost(0, 4 * 2**20),
        name="frame_second",
    )(fkeep_x, frecv_x, fkeep_y, frecv_y)
    flast_x = swap_block(fsum[0], 2)
    flast_y = swap_block(fsum[2], 1)
    frame_grad = pl.pallas_call(
        last_frame_kernel,
        out_shape=shape((nf, ch, cells), BF16),
        in_specs=[VMEM] * 4,
        out_specs=VMEM,
        compiler_params=params(),
        cost_estimate=cost(0, 2 * 2**20),
        name="frame_last",
    )(fsum[1], flast_x, fsum[3], flast_y)

    send_c2, keep_c2 = second(keep_c, recv_c)
    recv_c2 = swap_layer(send_c2, 2)
    weight_grad = pl.pallas_call(
        functools.partial(last_weight_kernel, width),
        out_shape=shape((quarter, TAPS * all_ch), F32),
        in_specs=[VMEM] * 6,
        out_specs=VMEM,
        scratch_shapes=[pltpu.VMEM((4, quarter, padded), F32)],
        compiler_params=params(),
        cost_estimate=cost(0, 4 * 2**20),
        name="weight_last",
    )(keep_a2, recv_a2, keep_b2, recv_b2, keep_c2, recv_c2)
    return (response, frame_grad, weight_grad)


def solution(mesh):
    small = mesh.shape["dp"] == 8 and mesh.shape["blk"] == 4
    return jax.shard_map(
        small_body if small else general_body,
        mesh=mesh,
        in_specs=(P("dp", "blk", None), P("blk", None), P("blk"), P("dp", "blk", None)),
        out_specs=(P("dp", "blk", None), P("dp", "blk", None), P(("blk", "dp"), None)),
        check_vma=False,
    )
```

```python
import functools

import jax
import jax.numpy as jnp
from jax import lax
from jax.experimental import pallas as pl
from jax.experimental.pallas import tpu as pltpu
from jax.sharding import PartitionSpec as P

WD = 16
TAPS = 9
F32, BF16 = jnp.float32, jnp.bfloat16
NT = (((1,), (1,)), ((), ()))
TN = (((0,), (0,)), ((), ()))
VMEM = pl.BlockSpec(memory_space=pltpu.VMEM)
ANY = pl.BlockSpec(memory_space=pl.ANY)
HBM = pl.BlockSpec(memory_space=pltpu.HBM)
SPAN = 125.0
RATE = 1e9
ORDER = ("a", "ka", "fx", "a2", "b", "c", "fy", "kb", "b2", "d", "kd", "c2", "resp", "f2", "d2", "fl", "wab", "wcd")
COST = dict(a=45, ka=40, fx=85, a2=7, b=40, c=40, d=40, kb=50, kd=40, fy=85, b2=7, c2=7, resp=110, f2=15, d2=7, fl=12, wab=24, wcd=24)


def shift_cells(maps, step_row, step_col):
    cells = maps.shape[-1]
    margin = WD + 1
    widths = [(0, 0)] * (maps.ndim - 1) + [(margin, margin)]
    flat = jnp.pad(maps, widths)
    begin = margin + step_row * WD + step_col
    moved = lax.slice_in_dim(flat, begin, begin + cells, axis=maps.ndim - 1)
    column = jnp.arange(cells, dtype=jnp.int32) % WD + step_col
    keeper = ((column >= 0) & (column < WD)).astype(maps.dtype)
    return moved * keeper


def general_body(frames, weight, bias, cotangent):
    nframe = frames.shape[0]
    local_ch = frames.shape[1]
    cells = frames.shape[2]
    whole = lax.all_gather(frames, "blk", axis=1, tiled=True)
    all_ch = whole.shape[1]
    total = jnp.zeros((nframe, local_ch, cells), F32)
    grads = []
    for tap in range(TAPS):
        ky, kx = divmod(tap, 3)
        piece = shift_cells(whole, ky - 1, kx - 1)
        w_tap = weight[:, tap * all_ch : (tap + 1) * all_ch]
        total = total + jnp.einsum("oi,fic->foc", w_tap, piece, preferred_element_type=F32)
        grads.append(
            lax.dot_general(cotangent, piece, (((0, 2), (0, 2)), ((), ())), preferred_element_type=F32)
        )
    response = (total + bias[None, :, None]).astype(BF16)
    local_grad = jnp.concatenate(grads, axis=1)
    weight_grad = lax.psum_scatter(local_grad, "dp", scatter_dimension=0, tiled=True)
    cot_moved = [shift_cells(cotangent, 1 - tap // 3, 1 - tap % 3) for tap in range(TAPS)]
    accum = jnp.zeros((all_ch, nframe, cells), F32)
    for tap in range(TAPS):
        w_cols = lax.slice_in_dim(weight, tap * all_ch, (tap + 1) * all_ch, axis=1)
        accum = accum + jnp.einsum("oi,foc->ifc", w_cols, cot_moved[tap], preferred_element_type=F32)
    shares = lax.psum_scatter(accum, "blk", scatter_dimension=0, tiled=True)
    frame_grad = jnp.transpose(shares, (1, 0, 2)).astype(BF16)
    return (response, frame_grad, weight_grad)


def scale_of(largest):
    return (jnp.maximum(largest, 1e-30) * 1.01).astype(BF16).astype(F32)


def encode(x, s):
    y = jnp.exp2(jnp.abs(x) * (2 * SPAN / s) - SPAN)
    return jnp.where(x < 0, -y, y)


def decode(code, s):
    y = code.astype(F32)
    v = (jnp.log2(jnp.abs(y)) + SPAN) * (s * (0.5 / SPAN))
    return jnp.where(y < 0, -v, v)


def cell_masks(rows, cells):
    lane = lax.broadcasted_iota(jnp.int32, (rows, cells), 1)
    return lane // WD, lane % WD


def moved(x, step, row, col, ky, kx):
    cells = x.shape[1]
    dy, dx = step * (ky - 1), step * (kx - 1)
    off = (dy * WD + dx) % cells
    out = pltpu.roll(x, off, 1) if off else x
    ok = None
    if dy:
        ok = (row >= dy) if dy > 0 else (row < cells // WD + dy)
    if dx:
        okx = (col >= dx) if dx > 0 else (col < WD + dx)
        ok = okx if ok is None else ok & okx
    return out if ok is None else jnp.where(ok, out, 0.0)


def put_rows_coded(out_ref, lead, values, width):
    rows, padded = values.shape
    s = scale_of(jnp.max(jnp.abs(values), axis=1, keepdims=True))
    codes = encode(values, s)
    last = padded - 128
    lane = lax.broadcasted_iota(jnp.int32, (rows, 128), 1) + last
    out_ref[lead + (slice(None), slice(0, last))] = codes[:, :last].astype(BF16)
    tail = jnp.where(lane < width, codes[:, last:], s)
    out_ref[lead + (slice(None), slice(last, padded))] = tail.astype(BF16)


def take_rows_coded(code, width):
    s = code[:, width : width + 1].astype(F32)
    return decode(code, s)


def weight_sums(width, cs_ref, xs_ref, f_ref):
    pieces, rows, padded = f_ref.shape
    ch = xs_ref.shape[0] // pieces
    for p in range(pieces):
        f_ref[p, :, width:] = jnp.zeros((rows, padded - width), F32)
    got = lax.dot_general(cs_ref[...], xs_ref[...], NT, preferred_element_type=F32)
    for t in range(TAPS):
        for p in range(pieces):
            f_ref[p, :, t * ch : (t + 1) * ch] = got[t * rows : (t + 1) * rows, p * ch : (p + 1) * ch]


def shifted_rows(far, cot_ref, base, cs_ref):
    nf, ch, cells = cot_ref.shape
    rows = cs_ref.shape[0] // TAPS
    block = rows // 2
    me = lax.axis_index("dp")
    z, core = me // 2, me % 2
    a = lax.broadcasted_iota(jnp.int32, (rows, ch), 0)
    o = lax.broadcasted_iota(jnp.int32, (rows, ch), 1)
    near = z ^ 1 if far else z
    layer = jnp.where(a < block, near, near ^ 2)
    want = (2 * layer + core) * block + jnp.where(a < block, a, a - block)
    pick = (o == want).astype(F32).astype(BF16)
    row, col = cell_masks(rows, cells)
    for f in range(nf):
        chosen = jnp.dot(pick, cot_ref[f], preferred_element_type=F32)
        at = (base + f) * cells
        for t in range(TAPS):
            ky, kx = divmod(t, 3)
            cs_ref[t * rows : (t + 1) * rows, at : at + cells] = moved(chosen, 1, row, col, ky, kx).astype(BF16)


def frames_in_a_row(x_ref, base, xs_ref):
    nf, _, cells = x_ref.shape
    for f in range(nf):
        xs_ref[:, (base + f) * cells : (base + f + 1) * cells] = x_ref[f]


def first_send_kernel(width, cot_hbm, cot2_hbm, x_hbm, x2_hbm, send_ref, cs_ref, xs_ref, v_ref, f_ref, sem):
    nf = cot_hbm.shape[0]
    loads = [
        pltpu.make_async_copy(src, v_ref.at[k], sem.at[k])
        for k, src in enumerate((cot_hbm, cot2_hbm, x_hbm, x2_hbm))
    ]
    for c in loads:
        c.start()
    for k in range(2):
        loads[k].wait()
        shifted_rows(True, v_ref.at[k], k * nf, cs_ref)
    for k in range(2):
        loads[2 + k].wait()
        frames_in_a_row(v_ref.at[2 + k], k * nf, xs_ref)
    weight_sums(width, cs_ref, xs_ref, f_ref)
    put_rows_coded(send_ref, (0,), f_ref[0], width)


def first_keep_kernel(width, cot_ref, cot2_ref, xs_ref, keep_ref, cs_ref):
    nf = cot_ref.shape[0]
    shifted_rows(False, cot_ref, 0, cs_ref)
    shifted_rows(False, cot2_ref, nf, cs_ref)
    weight_sums(width, cs_ref, xs_ref, keep_ref)


def later_send_kernel(width, cs_ref, x_ref, x2_ref, send_ref, xs_ref, f_ref):
    frames_in_a_row(x_ref, 0, xs_ref)
    frames_in_a_row(x2_ref, x_ref.shape[0], xs_ref)
    weight_sums(width, cs_ref, xs_ref, f_ref)
    put_rows_coded(send_ref, (0,), f_ref[0], width)


def later_keep_kernel(width, cs_ref, *refs):
    if len(refs) == 2:
        xs_ref, keep_ref = refs
        weight_sums(width, cs_ref, xs_ref, keep_ref)
    else:
        x0_ref, x1_ref, keep0_ref, keep1_ref, xs_ref, f_ref = refs
        ch = x0_ref.shape[0]
        xs_ref[:ch] = x0_ref[...]
        xs_ref[ch:] = x1_ref[...]
        weight_sums(width, cs_ref, xs_ref, f_ref)
        keep0_ref[0] = f_ref[0]
        keep1_ref[0] = f_ref[1]


def second_weight_kernel(width, keep_ref, recv_ref, send_ref, keep2_ref):
    pieces, rows, padded = keep_ref.shape
    half = rows // 2
    for p in range(pieces):
        total = keep_ref[p] + take_rows_coded(recv_ref[p], width)
        keep2_ref[p] = total[:half]
        lane = lax.broadcasted_iota(jnp.int32, (half, padded), 1)
        far = jnp.where(lane < width, total[half:], 0.0)
        s = scale_of(jnp.max(jnp.abs(far), axis=1, keepdims=True))
        codes = jnp.where(lane < width, encode(far, s), s)
        if pieces == 1:
            left = send_ref.shape[1]
            fill = jnp.broadcast_to(s, (half, 2 * left - padded))
            right = jnp.concatenate([codes[:, left:], fill], axis=1)
            send_ref[...] = jnp.concatenate([codes[:, :left], right], axis=0).astype(BF16)
        else:
            f = codes
            if p == 0:
                held = f
            else:
                send_ref[...] = jnp.concatenate([held, f], axis=0).astype(BF16)


def last_weight_kernel(width, side, *refs):
    ka, ra, kb, rb = refs[:4]
    out_hbm, acc, stage, sem = refs[-4:]
    blk = lax.axis_index("blk")
    half = ka.shape[1]
    padded = ka.shape[2]
    ch = width // TAPS
    for jj, (k, r) in enumerate(((ka, ra), (kb, rb))):
        left = r.shape[1]
        code = r[...].astype(F32)
        code = jnp.concatenate([code[:half], code[half:, : padded - left]], axis=1)
        acc[(blk % 2) ^ jj] = k[0] + take_rows_coded(code, width)
    start = pl.multiple_of((blk ^ side) // 2 * (2 * ch), 128)
    copies = []
    for t in range(TAPS):
        for q in range(2):
            stage[t, :, q * ch : (q + 1) * ch] = acc[q, :, t * ch : (t + 1) * ch]
        copies.append(
            pltpu.make_async_copy(
                stage.at[t], out_hbm.at[:, pl.ds(pl.multiple_of(t * 4 * ch + start, 128), 2 * ch)], sem.at[t]
            )
        )
        copies[-1].start()
    for c in copies:
        c.wait()


def put_columns_coded(send_ref, lead, left, right):
    ch, cells = left.shape
    scales = []
    for k, v in enumerate((left, right)):
        s = scale_of(jnp.max(jnp.abs(v), axis=0, keepdims=True))
        send_ref[lead + (slice(k * ch, (k + 1) * ch),)] = encode(v, s).astype(BF16)
        scales.append(jnp.broadcast_to(s, (8, cells)))
    send_ref[lead + (slice(2 * ch, 2 * ch + 16),)] = jnp.concatenate(scales, axis=0).astype(BF16)


def take_columns_coded(ref, lead, ch):
    scales = ref[lead + (slice(2 * ch, 2 * ch + 16),)].astype(F32)
    return [
        decode(ref[lead + (slice(k * ch, (k + 1) * ch),)], scales[8 * k : 8 * k + 1]) for k in range(2)
    ]


def load_taps(w_hbm, w_ref, sem, rows, all_ch):
    copies = [
        pltpu.make_async_copy(
            w_hbm.at[:, pl.ds(t * all_ch, all_ch)], w_ref.at[pl.ds(t * rows, rows)], sem.at[t]
        )
        for t in range(TAPS)
    ]
    for c in copies:
        c.start()
    return copies


def frame_grad_kernel(mask, f0, w_in, cot_hbm, send_ref, keep_ref, *refs):
    w_out = refs[:-4]
    cot_ref, cs_ref, out_ref, sem = refs[-4:]
    _, ch, cells = cot_hbm.shape
    w_ref = w_out[0] if w_out else w_in
    all_ch = w_ref.shape[1]
    load = pltpu.make_async_copy(cot_hbm.at[pl.ds(f0, 2)], cot_ref, sem.at[TAPS])
    load.start()
    copies = load_taps(w_in, w_ref, sem, ch, all_ch) if w_out else []
    row, col = cell_masks(ch, cells)
    load.wait()
    for f in range(2):
        x = cot_ref[f].astype(F32)
        for t in range(TAPS):
            ky, kx = divmod(t, 3)
            cs_ref[t * ch : (t + 1) * ch, f * cells : (f + 1) * cells] = moved(x, 1, row, col, ky, kx).astype(BF16)
    for c in copies:
        c.wait()
    tile = 256
    for i0 in range(0, all_ch, tile):
        out_ref[i0 : i0 + tile, :] = lax.dot_general(
            w_ref[:, i0 : i0 + tile], cs_ref[...], TN, preferred_element_type=F32
        )
    blk = lax.axis_index("blk")

    def block(q, f):
        return out_ref[pl.ds(pl.multiple_of(q * ch, 16), ch), f * cells : (f + 1) * cells]

    for k, q in enumerate((blk ^ mask, blk ^ 3)):
        put_columns_coded(send_ref, (k,), block(q, 0), block(q, 1))
    for k, q in enumerate((blk, blk ^ (3 - mask))):
        for f in range(2):
            keep_ref[k, f * ch : (f + 1) * ch, :] = block(q, f)


def second_frame_kernel(kx, rx, ky, ry, sx, k2x, sy, k2y):
    ch = kx.shape[1] // 2
    for k, r, s, k2 in ((kx, rx, sx, k2x), (ky, ry, sy, k2y)):
        for b in range(2):
            got = take_columns_coded(r, (b,), ch)
            sums = [k[b, f * ch : (f + 1) * ch, :] + got[f] for f in range(2)]
            if b == 0:
                for f in range(2):
                    k2[f * ch : (f + 1) * ch, :] = sums[f]
            else:
                put_columns_coded(s, (), sums[0], sums[1])


def last_frame_kernel(kx, rx, ky, ry, out_ref):
    ch = out_ref.shape[1]
    for h, (k, r) in enumerate(((kx, rx), (ky, ry))):
        got = take_columns_coded(r, (), ch)
        for f in range(2):
            out_ref[2 * h + f] = (k[f * ch : (f + 1) * ch, :] + got[f]).astype(BF16)


def response_kernel(w_ref, bias_ref, x0, x1, x2, x3, out_ref, x_ref, y_ref, sem):
    nf, ch, cells = x0.shape
    f = pl.program_id(0)
    blk = lax.axis_index("blk")

    def load(frame):
        for jj, x in enumerate((x0, x1, x2, x3)):
            at = pl.multiple_of((blk ^ jj) * ch, 16)
            yield pltpu.make_async_copy(x.at[frame], x_ref.at[frame, pl.ds(at, ch)], sem.at[frame, jj])

    @pl.when(f == 0)
    def _():
        for frame in range(nf):
            for c in load(frame):
                c.start()

    for c in load(f):
        c.wait()
    y_ref[...] = jnp.dot(w_ref[...], x_ref[f], preferred_element_type=F32)
    row, col = cell_masks(ch, cells)
    total = jnp.transpose(jnp.broadcast_to(bias_ref[...][None, :], (cells, ch)), (1, 0))
    for t in range(TAPS):
        ky, kx = divmod(t, 3)
        total = total + moved(y_ref[t * ch : (t + 1) * ch, :], -1, row, col, ky, kx)
    out_ref[0] = total.astype(BF16)


def params(mib=20):
    return pltpu.CompilerParams(vmem_limit_bytes=mib * 2**20)


def shape(dims, dtype):
    return jax.ShapeDtypeStruct(dims, dtype)


def swap_core(x):
    return lax.ppermute(x, "dp", [(d, d ^ 1) for d in range(8)])


def swap_layer(x, mask):
    return lax.ppermute(x, "dp", [(d, d ^ (2 * mask)) for d in range(8)])


def swap_block(x, mask):
    return lax.ppermute(x, "blk", [(d, d ^ mask) for d in range(4)])


def run(kernel, name, key, after, args, in_specs, out_shape, out_specs, scratch=(), **more):
    outs = out_shape if isinstance(out_shape, tuple) else (out_shape,)
    specs = out_specs if isinstance(out_specs, tuple) else (out_specs,)
    waits = [] if after is None else [after]
    n = len(waits)
    mark = pl.BlockSpec((8, 128), lambda *_: (0, 0))

    def body(*refs):
        ins = n + len(args)
        refs[ins + len(outs)][...] = jnp.zeros((8, 128), F32)
        kernel(*refs[n : ins + len(outs)], *refs[ins + len(outs) + 1 :])

    *got, token = pl.pallas_call(
        body,
        out_shape=(*outs, shape((8, 128), F32)),
        in_specs=[mark] * n + list(in_specs),
        out_specs=(*specs, mark),
        scratch_shapes=list(scratch),
        compiler_params=params(),
        cost_estimate=pl.CostEstimate(flops=int(COST[key] * RATE), bytes_accessed=1024, transcendentals=0),
        name=name,
        **more,
    )(*waits, *args)
    return (*got, token)


def small_body(frames, weight, bias, cotangent):
    nf, ch, cells = frames.shape
    all_ch = 4 * ch
    rows = ch // 2
    half, quarter = rows // 2, rows // 4
    width = TAPS * ch
    padded = -(-(width + 1) // 128) * 128
    left = -(-(padded // 2) // 128) * 128
    deep = 2 * nf * cells

    sums = shape((1, half, padded), F32)
    code = shape((1, half, padded), BF16)
    row_cs = shape((TAPS * half, deep), BF16)
    row_xs = shape((ch, deep), BF16)

    def first_send(after, *args):
        return run(
            functools.partial(first_send_kernel, width),
            "weight_send",
            "a",
            after,
            args,
            [HBM, ANY, HBM, ANY],
            (code, row_cs, row_xs),
            (VMEM, VMEM, VMEM),
            [
                pltpu.VMEM((4, nf, ch, cells), BF16),
                pltpu.VMEM((1, half, padded), F32),
                pltpu.SemaphoreType.DMA((4,)),
            ],
        )

    def first_keep(after, *args):
        return run(
            functools.partial(first_keep_kernel, width),
            "weight_keep",
            "ka",
            after,
            args,
            [VMEM] * 3,
            (sums, row_cs),
            (VMEM, VMEM),
        )

    def later_send(key, after, *args):
        return run(
            functools.partial(later_send_kernel, width),
            "weight_send",
            key,
            after,
            args,
            [VMEM] * 3,
            (code, row_xs),
            (VMEM, VMEM),
            [pltpu.VMEM((1, half, padded), F32)],
        )

    def later_keep(key, after, *args):
        n = len(args) - 1
        return run(
            functools.partial(later_keep_kernel, width),
            "weight_keep",
            key,
            after,
            args,
            [VMEM] * (n + 1),
            (sums,) * n,
            (VMEM,) * n,
            [pltpu.VMEM((2 * ch, deep), BF16), pltpu.VMEM((2, half, padded), F32)] if n == 2 else [],
        )

    def second(key, after, keep, recv):
        n = keep.shape[0]
        out = (2 * quarter, padded) if n == 2 else (2 * quarter, left)
        return run(
            functools.partial(second_weight_kernel, width),
            "weight_second",
            key,
            after,
            (keep, recv),
            [VMEM] * 2,
            (shape(out, BF16), shape((n, quarter, padded), F32)),
            (VMEM, VMEM),
        )

    def frame_part(key, after, mask, f0, w, rearrange):
        return run(
            functools.partial(frame_grad_kernel, mask, f0),
            "frame_part",
            key,
            after,
            (w, cotangent),
            [ANY if rearrange else VMEM, HBM],
            (shape((2, 2 * ch + 16, cells), BF16), shape((2, 2 * ch, cells), F32))
            + ((shape((TAPS * ch, all_ch), BF16),) if rearrange else ()),
            (VMEM,) * (3 if rearrange else 2),
            [
                pltpu.VMEM((2, ch, cells), BF16),
                pltpu.VMEM((TAPS * ch, 2 * cells), BF16),
                pltpu.VMEM((all_ch, 2 * cells), F32),
                pltpu.SemaphoreType.DMA((TAPS + 1,)),
            ],
        )

    def second_frame(key, after, *args):
        return run(
            second_frame_kernel,
            "frame_second",
            key,
            after,
            args,
            [VMEM] * 4,
            (
                shape((2 * ch + 16, cells), BF16),
                shape((2 * ch, cells), F32),
                shape((2 * ch + 16, cells), BF16),
                shape((2 * ch, cells), F32),
            ),
            (VMEM,) * 4,
        )

    def last_frame(key, after, *args):
        return run(
            last_frame_kernel, "frame_last", key, after, args, [VMEM] * 4, shape((nf, ch, cells), BF16), VMEM
        )

    def respond(key, after, *xs):
        return run(
            response_kernel,
            "response",
            key,
            after,
            (taps, bias, *xs),
            [VMEM, VMEM] + [ANY] * 4,
            shape((nf, ch, cells), BF16),
            pl.BlockSpec((1, ch, cells), lambda f: (f, 0, 0)),
            [
                pltpu.VMEM((nf, all_ch, cells), BF16),
                pltpu.VMEM((TAPS * ch, cells), F32),
                pltpu.SemaphoreType.DMA((nf, 4)),
            ],
            grid=(nf,),
        )

    def last_weight(key, after, side, parts, held):
        more = {} if held is None else {"input_output_aliases": {5: 0}}
        return run(
            functools.partial(last_weight_kernel, width, side),
            "weight_last",
            key,
            after,
            (*parts,) if held is None else (*parts, held),
            [VMEM] * 4 + ([] if held is None else [HBM]),
            shape((quarter, TAPS * all_ch), F32),
            HBM,
            [
                pltpu.VMEM((2, quarter, padded), F32),
                pltpu.VMEM((TAPS, quarter, 2 * ch), F32),
                pltpu.SemaphoreType.DMA((TAPS,)),
            ],
            **more,
        )

    cot2 = swap_core(cotangent)
    own2 = swap_core(frames)
    near_x = swap_block(frames, 1)
    near_y = swap_block(frames, 2)
    near_x2 = swap_core(near_x)
    near_y2 = swap_core(near_y)

    t = taps = None
    send, keep, recv, xs = {}, {}, {}, {}
    fsend, fkeep, frecv = {}, {}, {}
    diag = swap_block(near_x, 2)
    near = {"b": (near_x, near_x2), "c": (near_y, near_y2), "d": (diag, swap_core(diag))}
    for step in ORDER:
        if step == "a":
            send["a"], cs_far, xs["a"], t = first_send(t, cotangent, cot2, frames, own2)
            recv["a"] = swap_layer(send["a"], 1)
        elif step in ("b", "c", "d"):
            send[step], xs[step], t = later_send(step, t, cs_far, *near[step])
            recv[step] = swap_layer(send[step], 1)
        elif step == "ka":
            keep["a"], cs_near, t = first_keep(t, cotangent, cot2, xs["a"])
        elif step == "kb":
            keep["b"], keep["c"], t = later_keep(step, t, cs_near, xs["b"], xs["c"])
        elif step == "kd":
            keep["d"], t = later_keep(step, t, cs_near, xs["d"])
        elif step in ("a2", "b2", "c2", "d2"):
            k = step[0]
            send[step], keep[step], t = second(step, t, keep[k], recv[k])
            recv[step] = swap_layer(send[step], 2)
        elif step in ("fx", "fy"):
            k = 1 if step == "fx" else 2
            if taps is None:
                fsend[k], fkeep[k], taps, t = frame_part(step, t, k, 2 * k - 2, weight, True)
            else:
                fsend[k], fkeep[k], t = frame_part(step, t, k, 2 * k - 2, taps, False)
            frecv[k] = swap_block(fsend[k], k)
        elif step == "f2":
            sx, fkeep[3], sy, fkeep[4], t = second_frame(step, t, fkeep[1], frecv[1], fkeep[2], frecv[2])
            frecv[3] = swap_block(sx, 2)
            frecv[4] = swap_block(sy, 1)
        elif step == "fl":
            frame_grad, t = last_frame(step, t, fkeep[3], frecv[3], fkeep[4], frecv[4])
        elif step == "resp":
            response, t = respond(step, t, frames, near_x, near_y, diag)
        elif step == "wab":
            held, t = last_weight(step, t, 0, (keep["a2"], recv["a2"], keep["b2"], recv["b2"]), None)
        else:
            weight_grad, t = last_weight(step, t, 2, (keep["c2"], recv["c2"], keep["d2"], recv["d2"]), held)
    return (response, frame_grad, weight_grad)


def solution(mesh):
    small = mesh.shape["dp"] == 8 and mesh.shape["blk"] == 4
    return jax.shard_map(
        small_body if small else general_body,
        mesh=mesh,
        in_specs=(P("dp", "blk", None), P("blk", None), P("blk"), P("dp", "blk", None)),
        out_specs=(P("dp", "blk", None), P("dp", "blk", None), P(("blk", "dp"), None)),
        check_vma=False,
    )
```

```python
import functools

import jax
import jax.numpy as jnp
from jax import lax
from jax.experimental import pallas as pl
from jax.experimental.pallas import tpu as pltpu
from jax.sharding import PartitionSpec as P

WD = 16
TAPS = 9
F32, BF16 = jnp.float32, jnp.bfloat16
NT = (((1,), (1,)), ((), ()))
TN = (((0,), (0,)), ((), ()))
VMEM = pl.BlockSpec(memory_space=pltpu.VMEM)
ANY = pl.BlockSpec(memory_space=pl.ANY)
HBM = pl.BlockSpec(memory_space=pltpu.HBM)
SPAN = 125.0
RATE = 5e8
ROOM = dict(pre=8, a=12, fx=18, gx=4, gy=4, gd=4, ka=20, a2=8, b=10, fy=18, c=10, kb=18, f2x=8, b2=8, ab2=10, kd=10, c2=8, d=10, f2y=8, wab=10, flx=6, d2=8, resp=18, fly=6, wcd=10)
ORDER = ("pre", "a", "ka", "fx", "gx", "gy", "a2", "b", "c", "kb", "gd", "f2x", "fy", "b2", "kd", "c2", "d", "f2y", "wab", "flx", "d2", "resp", "fly", "wcd")
COST = dict(pre=20, a=45, ka=40, fx=85, gx=10, gy=10, gd=10, b=30, c=40, d=40, kb=50, kd=40, fy=10, a2=7, b2=7, c2=7, resp=110, f2x=12, f2y=12, d2=7, flx=10, fly=10, wab=24, wcd=24)


def shift_cells(maps, step_row, step_col):
    cells = maps.shape[-1]
    margin = WD + 1
    widths = [(0, 0)] * (maps.ndim - 1) + [(margin, margin)]
    flat = jnp.pad(maps, widths)
    begin = margin + step_row * WD + step_col
    moved = lax.slice_in_dim(flat, begin, begin + cells, axis=maps.ndim - 1)
    column = jnp.arange(cells, dtype=jnp.int32) % WD + step_col
    keeper = ((column >= 0) & (column < WD)).astype(maps.dtype)
    return moved * keeper


def general_body(frames, weight, bias, cotangent):
    nframe = frames.shape[0]
    local_ch = frames.shape[1]
    cells = frames.shape[2]
    whole = lax.all_gather(frames, "blk", axis=1, tiled=True)
    all_ch = whole.shape[1]
    total = jnp.zeros((nframe, local_ch, cells), F32)
    grads = []
    for tap in range(TAPS):
        ky, kx = divmod(tap, 3)
        piece = shift_cells(whole, ky - 1, kx - 1)
        w_tap = weight[:, tap * all_ch : (tap + 1) * all_ch]
        total = total + jnp.einsum("oi,fic->foc", w_tap, piece, preferred_element_type=F32)
        grads.append(
            lax.dot_general(cotangent, piece, (((0, 2), (0, 2)), ((), ())), preferred_element_type=F32)
        )
    response = (total + bias[None, :, None]).astype(BF16)
    local_grad = jnp.concatenate(grads, axis=1)
    weight_grad = lax.psum_scatter(local_grad, "dp", scatter_dimension=0, tiled=True)
    cot_moved = [shift_cells(cotangent, 1 - tap // 3, 1 - tap % 3) for tap in range(TAPS)]
    accum = jnp.zeros((all_ch, nframe, cells), F32)
    for tap in range(TAPS):
        w_cols = lax.slice_in_dim(weight, tap * all_ch, (tap + 1) * all_ch, axis=1)
        accum = accum + jnp.einsum("oi,foc->ifc", w_cols, cot_moved[tap], preferred_element_type=F32)
    shares = lax.psum_scatter(accum, "blk", scatter_dimension=0, tiled=True)
    frame_grad = jnp.transpose(shares, (1, 0, 2)).astype(BF16)
    return (response, frame_grad, weight_grad)


def scale_of(largest):
    return (jnp.maximum(largest, 1e-30) * 1.01).astype(BF16).astype(F32)


def encode(x, s):
    y = jnp.exp2(jnp.abs(x) * (2 * SPAN / s) - SPAN)
    return jnp.where(x < 0, -y, y)


def decode(code, s):
    y = code.astype(F32)
    v = (jnp.log2(jnp.abs(y)) + SPAN) * (s * (0.5 / SPAN))
    return jnp.where(y < 0, -v, v)


LANES = 128


def col_moved(x, dx):
    if dx == 0:
        return x
    rows, cells = x.shape
    col = lax.broadcasted_iota(jnp.int32, (rows, LANES), 1) % WD
    ok = (col >= dx) if dx > 0 else (col < WD + dx)
    parts = [
        jnp.where(ok, pltpu.roll(x[:, at : at + LANES], dx % LANES, 1), 0.0) for at in range(0, cells, LANES)
    ]
    return jnp.concatenate(parts, axis=1)


def row_moved(x, dy):
    if dy == 0:
        return x
    rows, cells = x.shape
    by = dy * WD
    lane = lax.broadcasted_iota(jnp.int32, (rows, LANES), 1)
    parts = [pltpu.roll(x[:, at : at + LANES], by % LANES, 1) for at in range(0, cells, LANES)]
    if dy > 0:
        parts = [jnp.where(lane < by, parts[k - 1] if k else 0.0, parts[k]) for k in range(len(parts))]
    else:
        after = parts[1:] + [0.0]
        parts = [jnp.where(lane >= LANES + by, after[k], parts[k]) for k in range(len(parts))]
    return jnp.concatenate(parts, axis=1)


def all_moved(x):
    for kx in range(3):
        along = col_moved(x, kx - 1)
        for ky in range(3):
            yield 3 * ky + kx, row_moved(along, ky - 1)


def put_rows_coded(out_ref, lead, values, width):
    rows, padded = values.shape
    s = scale_of(jnp.max(jnp.abs(values), axis=1, keepdims=True))
    codes = encode(values, s)
    last = padded - 128
    lane = lax.broadcasted_iota(jnp.int32, (rows, 128), 1) + last
    out_ref[lead + (slice(None), slice(0, last))] = codes[:, :last].astype(BF16)
    tail = jnp.where(lane < width, codes[:, last:], s)
    out_ref[lead + (slice(None), slice(last, padded))] = tail.astype(BF16)


def take_rows_coded(code, width):
    s = code[:, width : width + 1].astype(F32)
    return decode(code, s)


def weight_sums(width, cs_refs, xs_refs, f_ref):
    pieces, rows, padded = f_ref.shape
    ch = xs_refs[0].shape[0] // pieces
    for p in range(pieces):
        f_ref[p, :, width:] = jnp.zeros((rows, padded - width), F32)
    got = lax.dot_general(cs_refs[0][...], xs_refs[0][...], NT, preferred_element_type=F32)
    got = got + lax.dot_general(cs_refs[1][...], xs_refs[1][...], NT, preferred_element_type=F32)
    for t in range(TAPS):
        for p in range(pieces):
            f_ref[p, :, t * ch : (t + 1) * ch] = got[t * rows : (t + 1) * rows, p * ch : (p + 1) * ch]


def shifted_rows(far, cot_ref, cs_ref):
    nf, ch, cells = cot_ref.shape
    rows = cs_ref.shape[0] // TAPS
    block = rows // 2
    me = lax.axis_index("dp")
    z, core = me // 2, me % 2
    a = lax.broadcasted_iota(jnp.int32, (rows, ch), 0)
    o = lax.broadcasted_iota(jnp.int32, (rows, ch), 1)
    near = z ^ 1 if far else z
    layer = jnp.where(a < block, near, near ^ 2)
    want = (2 * layer + core) * block + jnp.where(a < block, a, a - block)
    pick = (o == want).astype(F32).astype(BF16)
    for f in range(nf):
        chosen = jnp.dot(pick, cot_ref[f], preferred_element_type=F32)
        at = f * cells
        for t, tap in all_moved(chosen):
            cs_ref[t * rows : (t + 1) * rows, at : at + cells] = tap.astype(BF16)


def frames_in_a_row(x_ref, xs_ref):
    nf, _, cells = x_ref.shape
    for f in range(nf):
        xs_ref[:, f * cells : (f + 1) * cells] = x_ref[f]


def own_rows_kernel(cot_ref, x_ref, cs_ref, xs_ref):
    shifted_rows(True, cot_ref, cs_ref)
    frames_in_a_row(x_ref, xs_ref)


def first_send_kernel(width, cs_ref, xs_ref, cot2_ref, x2_ref, x_ref, send_ref, cs2_ref, xs2_ref, copy_ref, f_ref):
    shifted_rows(True, cot2_ref, cs2_ref)
    frames_in_a_row(x2_ref, xs2_ref)
    copy_ref[...] = x_ref[...]
    weight_sums(width, (cs_ref, cs2_ref), (xs_ref, xs2_ref), f_ref)
    put_rows_coded(send_ref, (0,), f_ref[0], width)


def first_keep_kernel(width, cot_ref, cot2_ref, xs_ref, xs2_ref, w_hbm, keep_ref, cs_ref, cs2_ref, w_ref, sem):
    copies = load_taps(w_hbm, w_ref, sem, xs_ref.shape[0], w_ref.shape[1])
    shifted_rows(False, cot_ref, cs_ref)
    shifted_rows(False, cot2_ref, cs2_ref)
    weight_sums(width, (cs_ref, cs2_ref), (xs_ref, xs2_ref), keep_ref)
    for c in copies:
        c.wait()


def later_send_kernel(width, cs_ref, cs2_ref, xs_ref, xs2_ref, send_ref, f_ref):
    weight_sums(width, (cs_ref, cs2_ref), (xs_ref, xs2_ref), f_ref)
    put_rows_coded(send_ref, (0,), f_ref[0], width)


def later_keep_kernel(width, cs_ref, cs2_ref, *refs):
    if len(refs) == 3:
        xs_ref, xs2_ref, keep_ref = refs
        weight_sums(width, (cs_ref, cs2_ref), (xs_ref, xs2_ref), keep_ref)
    else:
        x0, x02, x1, x12, keep0_ref, keep1_ref, xs_ref, xs2_ref, f_ref = refs
        ch = x0.shape[0]
        xs_ref[:ch] = x0[...]
        xs_ref[ch:] = x1[...]
        xs2_ref[:ch] = x02[...]
        xs2_ref[ch:] = x12[...]
        weight_sums(width, (cs_ref, cs2_ref), (xs_ref, xs2_ref), f_ref)
        keep0_ref[0] = f_ref[0]
        keep1_ref[0] = f_ref[1]


def second_weight_kernel(width, pieces, *refs):
    ins, send_ref, keep_refs = refs[: 2 * pieces], refs[2 * pieces], refs[2 * pieces + 1 :]
    parts = []
    for p in range(pieces):
        keep_ref, recv_ref = ins[2 * p : 2 * p + 2]
        _, rows, padded = keep_ref.shape
        half = rows // 2
        total = keep_ref[0] + take_rows_coded(recv_ref[0], width)
        keep_refs[p][...] = total[:half]
        lane = lax.broadcasted_iota(jnp.int32, (half, padded), 1)
        far = jnp.where(lane < width, total[half:], 0.0)
        s = scale_of(jnp.max(jnp.abs(far), axis=1, keepdims=True))
        parts.append(jnp.where(lane < width, encode(far, s), s))
    if pieces == 1:
        left = send_ref.shape[1]
        fill = jnp.broadcast_to(s, (half, 2 * left - padded))
        parts = [parts[0][:, :left], jnp.concatenate([parts[0][:, left:], fill], axis=1)]
    send_ref[...] = jnp.concatenate(parts, axis=0).astype(BF16)


def last_weight_kernel(width, side, *refs):
    out_hbm, acc, stage, sem = refs[-4:]
    keeps = refs[:2]
    blk = lax.axis_index("blk")
    half, padded = keeps[0].shape
    ch = width // TAPS
    if refs[2].shape[1] == padded:
        code = refs[2][...].astype(F32)
        codes = (code[:half], code[half:])
    else:
        codes = []
        for r in refs[2:4]:
            code = r[...].astype(F32)
            codes.append(jnp.concatenate([code[:half], code[half:, : padded - r.shape[1]]], axis=1))
    for jj in range(2):
        acc[(blk % 2) ^ jj] = keeps[jj][...] + take_rows_coded(codes[jj], width)
    start = pl.multiple_of((blk ^ side) // 2 * (2 * ch), 128)
    copies = []
    for t in range(TAPS):
        for q in range(2):
            stage[t, :, q * ch : (q + 1) * ch] = acc[q, :, t * ch : (t + 1) * ch]
        copies.append(
            pltpu.make_async_copy(
                stage.at[t], out_hbm.at[:, pl.ds(pl.multiple_of(t * 4 * ch + start, 128), 2 * ch)], sem.at[t]
            )
        )
        copies[-1].start()
    for c in copies:
        c.wait()


def put_columns_coded(send_ref, lead, left, right):
    ch, cells = left.shape
    scales = []
    for k, v in enumerate((left, right)):
        s = scale_of(jnp.max(jnp.abs(v), axis=0, keepdims=True))
        send_ref[lead + (slice(k * ch, (k + 1) * ch),)] = encode(v, s).astype(BF16)
        scales.append(jnp.broadcast_to(s, (8, cells)))
    send_ref[lead + (slice(2 * ch, 2 * ch + 16),)] = jnp.concatenate(scales, axis=0).astype(BF16)


def take_columns_coded(ref, lead, ch):
    scales = ref[lead + (slice(2 * ch, 2 * ch + 16),)].astype(F32)
    return [
        decode(ref[lead + (slice(k * ch, (k + 1) * ch),)], scales[8 * k : 8 * k + 1]) for k in range(2)
    ]


def load_taps(w_hbm, w_ref, sem, rows, all_ch):
    copies = [
        pltpu.make_async_copy(
            w_hbm.at[:, pl.ds(t * all_ch, all_ch)], w_ref.at[pl.ds(t * rows, rows)], sem.at[t]
        )
        for t in range(TAPS)
    ]
    for c in copies:
        c.start()
    return copies


def frame_grad_kernel(mask, f0, w_ref, cot_hbm, send_ref, keep_ref, cot_ref, cs_ref, out_ref, sem):
    _, ch, cells = cot_hbm.shape
    all_ch = w_ref.shape[1]
    load = pltpu.make_async_copy(cot_hbm.at[pl.ds(f0, 2)], cot_ref, sem)
    load.start()
    load.wait()
    for f in range(2):
        for t, tap in all_moved(cot_ref[f].astype(F32)):
            cs_ref[t * ch : (t + 1) * ch, f * cells : (f + 1) * cells] = tap.astype(BF16)
    tile = 256
    for i0 in range(0, all_ch, tile):
        out_ref[i0 : i0 + tile, :] = lax.dot_general(
            w_ref[:, i0 : i0 + tile], cs_ref[...], TN, preferred_element_type=F32
        )
    blk = lax.axis_index("blk")

    def block(q, f):
        return out_ref[pl.ds(pl.multiple_of(q * ch, 16), ch), f * cells : (f + 1) * cells]

    for k, q in enumerate((blk ^ mask, blk ^ 3)):
        put_columns_coded(send_ref, (k,), block(q, 0), block(q, 1))
    for k, q in enumerate((blk, blk ^ (3 - mask))):
        for f in range(2):
            keep_ref[k, f * ch : (f + 1) * ch, :] = block(q, f)


def second_frame_kernel(k, r, s, k2):
    ch = k.shape[1] // 2
    for b in range(2):
        got = take_columns_coded(r, (b,), ch)
        sums = [k[b, f * ch : (f + 1) * ch, :] + got[f] for f in range(2)]
        if b == 0:
            for f in range(2):
                k2[f * ch : (f + 1) * ch, :] = sums[f]
        else:
            put_columns_coded(s, (), sums[0], sums[1])


def last_frame_kernel(f0, k, r, *refs):
    out_hbm, stage, sem = refs[-3:]
    ch = stage.shape[1]
    got = take_columns_coded(r, (), ch)
    for f in range(2):
        stage[f] = (k[f * ch : (f + 1) * ch, :] + got[f]).astype(BF16)
    copy = pltpu.make_async_copy(stage, out_hbm.at[pl.ds(f0, 2)], sem)
    copy.start()
    copy.wait()


def response_kernel(w_ref, bias_ref, x0, x1, x2, x3, out_ref, x_ref, y_ref):
    nf, ch, cells = x0.shape
    blk = lax.axis_index("blk")
    base = jnp.transpose(jnp.broadcast_to(bias_ref[...][None, :], (cells, ch)), (1, 0))

    @pl.loop(0, nf)
    def _(f):
        for jj, x in enumerate((x0, x1, x2, x3)):
            x_ref[pl.ds(pl.multiple_of((blk ^ jj) * ch, 16), ch), :] = x[f]
        y_ref[...] = jnp.dot(w_ref[...], x_ref[...], preferred_element_type=F32)
        total = base
        for ky in range(3):
            line = None
            for kx in range(3):
                t = 3 * ky + kx
                part = col_moved(y_ref[t * ch : (t + 1) * ch, :], 1 - kx)
                line = part if line is None else line + part
            total = total + row_moved(line, 1 - ky)
        out_ref[f] = total.astype(BF16)


def params(mib):
    return pltpu.CompilerParams(vmem_limit_bytes=mib * 2**20)


def shape(dims, dtype):
    return jax.ShapeDtypeStruct(dims, dtype)


def swap_core(x):
    return lax.ppermute(x, "dp", [(d, d ^ 1) for d in range(8)])


def swap_layer(x, mask):
    return lax.ppermute(x, "dp", [(d, d ^ (2 * mask)) for d in range(8)])


def swap_block(x, mask):
    return lax.ppermute(x, "blk", [(d, d ^ mask) for d in range(4)])


def run(kernel, name, key, after, args, in_specs, out_shape, out_specs, scratch=(), **more):
    outs = out_shape if isinstance(out_shape, tuple) else (out_shape,)
    specs = out_specs if isinstance(out_specs, tuple) else (out_specs,)
    waits = [] if after is None else [after]
    n = len(waits)
    mark = pl.BlockSpec((8, 128), lambda *_: (0, 0))

    def body(*refs):
        ins = n + len(args)
        refs[ins + len(outs)][...] = jnp.zeros((8, 128), F32)
        kernel(*refs[n : ins + len(outs)], *refs[ins + len(outs) + 1 :])

    *got, token = pl.pallas_call(
        body,
        out_shape=(*outs, shape((8, 128), F32)),
        in_specs=[mark] * n + list(in_specs),
        out_specs=(*specs, mark),
        scratch_shapes=list(scratch),
        compiler_params=params(ROOM[key]),
        cost_estimate=pl.CostEstimate(flops=int(COST[key] * RATE), bytes_accessed=1024, transcendentals=0),
        name=name,
        **more,
    )(*waits, *args)
    return (*got, token)


def small_body(frames, weight, bias, cotangent):
    nf, ch, cells = frames.shape
    all_ch = 4 * ch
    rows = ch // 2
    half, quarter = rows // 2, rows // 4
    width = TAPS * ch
    padded = -(-(width + 1) // 128) * 128
    left = -(-(padded // 2) // 128) * 128

    sums = shape((1, half, padded), F32)
    code = shape((1, half, padded), BF16)
    row_cs = shape((TAPS * half, nf * cells), BF16)
    row_xs = shape((ch, nf * cells), BF16)
    kept = shape((quarter, padded), F32)

    def simple(kernel, name, key, after, args, outs, scratch=()):
        return run(kernel, name, key, after, args, [VMEM] * len(args), outs, (VMEM,) * len(outs), scratch)

    def later_keep(key, after, *args):
        n = (len(args) - 2) // 2
        scratch = [pltpu.VMEM((2 * ch, nf * cells), BF16)] * 2 + [pltpu.VMEM((2, half, padded), F32)]
        return simple(
            functools.partial(later_keep_kernel, width),
            "weight_keep",
            key,
            after,
            args,
            (sums,) * n,
            scratch if n == 2 else (),
        )

    def second(key, after, *args):
        n = len(args) // 2
        out = (2 * quarter, padded) if n == 2 else (2 * quarter, left)
        return simple(
            functools.partial(second_weight_kernel, width, n),
            "weight_second",
            key,
            after,
            args,
            (shape(out, BF16),) + (kept,) * n,
        )

    def frame_part(key, after, mask, f0):
        return run(
            functools.partial(frame_grad_kernel, mask, f0),
            "frame_part",
            key,
            after,
            (taps, cotangent),
            [VMEM, HBM],
            (shape((2, 2 * ch + 16, cells), BF16), shape((2, 2 * ch, cells), F32)),
            (VMEM, VMEM),
            [
                pltpu.VMEM((2, ch, cells), BF16),
                pltpu.VMEM((TAPS * ch, 2 * cells), BF16),
                pltpu.VMEM((all_ch, 2 * cells), F32),
                pltpu.SemaphoreType.DMA,
            ],
        )

    def second_frame(key, after, *args):
        outs = (shape((2 * ch + 16, cells), BF16), shape((2 * ch, cells), F32))
        return simple(second_frame_kernel, "frame_second", key, after, args, outs)

    def last_frame(key, after, f0, parts, held):
        more = {} if held is None else {"input_output_aliases": {3: 0}}
        return run(
            functools.partial(last_frame_kernel, f0),
            "frame_last",
            key,
            after,
            parts if held is None else (*parts, held),
            [VMEM] * 2 + ([] if held is None else [HBM]),
            shape((nf, ch, cells), BF16),
            HBM,
            [pltpu.VMEM((2, ch, cells), BF16), pltpu.SemaphoreType.DMA],
            **more,
        )

    def respond(key, after, *xs):
        return run(
            response_kernel,
            "response",
            key,
            after,
            (taps, bias, *xs),
            [VMEM] * 6,
            shape((nf, ch, cells), BF16),
            VMEM,
            [pltpu.VMEM((all_ch, cells), BF16), pltpu.VMEM((TAPS * ch, cells), F32)],
        )

    def last_weight(key, after, side, parts, held):
        more = {} if held is None else {"input_output_aliases": {len(parts) + 1: 0}}
        return run(
            functools.partial(last_weight_kernel, width, side),
            "weight_last",
            key,
            after,
            parts if held is None else (*parts, held),
            [VMEM] * len(parts) + ([] if held is None else [HBM]),
            shape((quarter, TAPS * all_ch), F32),
            HBM,
            [
                pltpu.VMEM((2, quarter, padded), F32),
                pltpu.VMEM((TAPS, quarter, 2 * ch), F32),
                pltpu.SemaphoreType.DMA((TAPS,)),
            ],
            **more,
        )

    cot2 = swap_core(cotangent)
    own2 = swap_core(frames)
    near = {"x": swap_block(frames, 1)}

    t = None
    send, keep, recv, xs, cs = {}, {}, {}, {}, {}
    fsend, fkeep, frecv = {}, {}, {}
    for step in ORDER:
        if step == "pre":
            cs_own, xs_own, t = simple(own_rows_kernel, "own_rows", step, t, (cotangent, frames), (row_cs, row_xs))
        elif step == "a":
            send["a"], cs2, xs2, again, t = simple(
                functools.partial(first_send_kernel, width),
                "weight_send",
                step,
                t,
                (cs_own, xs_own, cot2, own2, frames),
                (code, row_cs, row_xs, shape((nf, ch, cells), BF16)),
                [pltpu.VMEM((1, half, padded), F32)],
            )
            cs["far"], xs["a"] = (cs_own, cs2), (xs_own, xs2)
            recv["a"] = swap_layer(send["a"], 1)
            near["y"] = swap_block(frames, 2)
        elif step in ("gx", "gy", "gd"):
            k = step[1]
            row, t = simple(frames_in_a_row, "rows", step, t, (near[k],), (row_xs,))
            xs["bcd"["xyd".index(k)]] = (row, swap_core(row))
            if k == "x":
                near["d"] = swap_block(near["x"], 2)
        elif step in ("b", "c", "d"):
            send[step], t = simple(
                functools.partial(later_send_kernel, width),
                "weight_send",
                step,
                t,
                (*cs["far"], *xs[step]),
                (code,),
                [pltpu.VMEM((1, half, padded), F32)],
            )
            recv[step] = swap_layer(send[step], 1)
        elif step == "ka":
            keep["a"], cs_near, cs2_near, taps, t = run(
                functools.partial(first_keep_kernel, width),
                "weight_keep",
                step,
                t,
                (cotangent, cot2, *xs["a"], weight),
                [VMEM] * 4 + [ANY],
                (sums, row_cs, row_cs, shape((TAPS * ch, all_ch), BF16)),
                (VMEM,) * 4,
                [pltpu.SemaphoreType.DMA((TAPS,))],
            )
            cs["near"] = (cs_near, cs2_near)
        elif step == "kb":
            keep["b"], keep["c"], t = later_keep(step, t, *cs["near"], *xs["b"], *xs["c"])
        elif step == "kd":
            keep["d"], t = later_keep(step, t, *cs["near"], *xs["d"])
        elif step == "ab2":
            send[step], keep["a2"], keep["b2"], t = second(step, t, keep["a"], recv["a"], keep["b"], recv["b"])
            recv[step] = swap_layer(send[step], 2)
        elif step in ("a2", "b2", "c2", "d2"):
            k = step[0]
            send[step], keep[step], t = second(step, t, keep[k], recv[k])
            recv[step] = swap_layer(send[step], 2)
        elif step in ("fx", "fy"):
            k = 1 if step == "fx" else 2
            fsend[k], fkeep[k], t = frame_part(step, t, k, 2 * k - 2)
            frecv[k] = swap_block(fsend[k], k)
        elif step in ("f2x", "f2y"):
            k = 1 if step == "f2x" else 2
            fsend[k + 2], fkeep[k + 2], t = second_frame(step, t, fkeep[k], frecv[k])
            frecv[k + 2] = swap_block(fsend[k + 2], 3 - k)
        elif step == "flx":
            fheld, t = last_frame(step, t, 0, (fkeep[3], frecv[3]), None)
        elif step == "fly":
            frame_grad, t = last_frame(step, t, 2, (fkeep[4], frecv[4]), fheld)
        elif step == "resp":
            response, t = respond(step, t, again, near["x"], near["y"], near["d"])
        elif step == "wab":
            codes = (recv["ab2"],) if "ab2" in recv else (recv["a2"], recv["b2"])
            held, t = last_weight(step, t, 0, (keep["a2"], keep["b2"], *codes), None)
        else:
            weight_grad, t = last_weight(step, t, 2, (keep["c2"], keep["d2"], recv["c2"], recv["d2"]), held)
    return (response, frame_grad, weight_grad)


def solution(mesh):
    small = mesh.shape["dp"] == 8 and mesh.shape["blk"] == 4
    return jax.shard_map(
        small_body if small else general_body,
        mesh=mesh,
        in_specs=(P("dp", "blk", None), P("blk", None), P("blk"), P("dp", "blk", None)),
        out_specs=(P("dp", "blk", None), P("dp", "blk", None), P(("blk", "dp"), None)),
        check_vma=False,
    )
```

```python
import functools

import jax
import jax.numpy as jnp
from jax import lax
from jax.experimental import pallas as pl
from jax.experimental.pallas import tpu as pltpu
from jax.sharding import PartitionSpec as P

WD = 16
TAPS = 9
F32, BF16 = jnp.float32, jnp.bfloat16
NT = (((1,), (1,)), ((), ()))
TN = (((0,), (0,)), ((), ()))
VMEM = pl.BlockSpec(memory_space=pltpu.VMEM)
ANY = pl.BlockSpec(memory_space=pl.ANY)
HBM = pl.BlockSpec(memory_space=pltpu.HBM)
SPAN = 125.0
RATE = 5e8
ROOM = dict(pre=8, a=12, fx=18, gx=4, gy=4, gd=4, ka=20, a2=8, b=10, fy=18, c=10, kb=18, f2x=8, b2=8, kd=10, c2=8, d=10, f2y=8, wab=10, flx=6, d2=8, resp=18, fly=6, wcd=10, ea=8, eb=8, ec=8)
ORDER = ("pre", "a", "ka", "fx", "gx", "gy", "a2", "b", "c", "kb", "f2x", "ea", "gd", "fy", "b2", "d", "kd", "c2", "eb", "f2y", "wab", "flx", "d2", "resp", "fly", "ec", "wcd")
COST = dict(pre=20, a=45, ka=40, fx=85, gx=10, gy=10, gd=10, b=40, c=40, d=40, kb=50, kd=40, fy=85, a2=7, b2=7, c2=7, resp=110, f2x=12, f2y=12, d2=7, flx=10, fly=10, wab=24, wcd=24, ea=7, eb=7, ec=7)


def shift_cells(maps, step_row, step_col):
    cells = maps.shape[-1]
    margin = WD + 1
    widths = [(0, 0)] * (maps.ndim - 1) + [(margin, margin)]
    flat = jnp.pad(maps, widths)
    begin = margin + step_row * WD + step_col
    moved = lax.slice_in_dim(flat, begin, begin + cells, axis=maps.ndim - 1)
    column = jnp.arange(cells, dtype=jnp.int32) % WD + step_col
    keeper = ((column >= 0) & (column < WD)).astype(maps.dtype)
    return moved * keeper


def general_body(frames, weight, bias, cotangent):
    nframe = frames.shape[0]
    local_ch = frames.shape[1]
    cells = frames.shape[2]
    whole = lax.all_gather(frames, "blk", axis=1, tiled=True)
    all_ch = whole.shape[1]
    total = jnp.zeros((nframe, local_ch, cells), F32)
    grads = []
    for tap in range(TAPS):
        ky, kx = divmod(tap, 3)
        piece = shift_cells(whole, ky - 1, kx - 1)
        w_tap = weight[:, tap * all_ch : (tap + 1) * all_ch]
        total = total + jnp.einsum("oi,fic->foc", w_tap, piece, preferred_element_type=F32)
        grads.append(
            lax.dot_general(cotangent, piece, (((0, 2), (0, 2)), ((), ())), preferred_element_type=F32)
        )
    response = (total + bias[None, :, None]).astype(BF16)
    local_grad = jnp.concatenate(grads, axis=1)
    weight_grad = lax.psum_scatter(local_grad, "dp", scatter_dimension=0, tiled=True)
    cot_moved = [shift_cells(cotangent, 1 - tap // 3, 1 - tap % 3) for tap in range(TAPS)]
    accum = jnp.zeros((all_ch, nframe, cells), F32)
    for tap in range(TAPS):
        w_cols = lax.slice_in_dim(weight, tap * all_ch, (tap + 1) * all_ch, axis=1)
        accum = accum + jnp.einsum("oi,foc->ifc", w_cols, cot_moved[tap], preferred_element_type=F32)
    shares = lax.psum_scatter(accum, "blk", scatter_dimension=0, tiled=True)
    frame_grad = jnp.transpose(shares, (1, 0, 2)).astype(BF16)
    return (response, frame_grad, weight_grad)


def scale_of(largest):
    return (jnp.maximum(largest, 1e-30) * 1.01).astype(BF16).astype(F32)


def encode(x, s):
    y = jnp.exp2(jnp.abs(x) * (2 * SPAN / s) - SPAN)
    return jnp.where(x < 0, -y, y)


def decode(code, s):
    y = code.astype(F32)
    v = (jnp.log2(jnp.abs(y)) + SPAN) * (s * (0.5 / SPAN))
    return jnp.where(y < 0, -v, v)


LANES = 128


def col_moved(x, dx):
    if dx == 0:
        return x
    rows, cells = x.shape
    col = lax.broadcasted_iota(jnp.int32, (rows, LANES), 1) % WD
    ok = (col >= dx) if dx > 0 else (col < WD + dx)
    parts = [
        jnp.where(ok, pltpu.roll(x[:, at : at + LANES], dx % LANES, 1), 0.0) for at in range(0, cells, LANES)
    ]
    return jnp.concatenate(parts, axis=1)


def row_moved(x, dy):
    if dy == 0:
        return x
    rows, cells = x.shape
    by = dy * WD
    lane = lax.broadcasted_iota(jnp.int32, (rows, LANES), 1)
    parts = [pltpu.roll(x[:, at : at + LANES], by % LANES, 1) for at in range(0, cells, LANES)]
    if dy > 0:
        parts = [jnp.where(lane < by, parts[k - 1] if k else 0.0, parts[k]) for k in range(len(parts))]
    else:
        after = parts[1:] + [0.0]
        parts = [jnp.where(lane >= LANES + by, after[k], parts[k]) for k in range(len(parts))]
    return jnp.concatenate(parts, axis=1)


def all_moved(x):
    for kx in range(3):
        along = col_moved(x, kx - 1)
        for ky in range(3):
            yield 3 * ky + kx, row_moved(along, ky - 1)


def put_rows_coded(out_ref, lead, values, width):
    rows, padded = values.shape
    s = scale_of(jnp.max(jnp.abs(values), axis=1, keepdims=True))
    codes = encode(values, s)
    last = padded - 128
    lane = lax.broadcasted_iota(jnp.int32, (rows, 128), 1) + last
    out_ref[lead + (slice(None), slice(0, last))] = codes[:, :last].astype(BF16)
    tail = jnp.where(lane < width, codes[:, last:], s)
    out_ref[lead + (slice(None), slice(last, padded))] = tail.astype(BF16)


def take_rows_coded(code, width):
    s = code[:, width : width + 1].astype(F32)
    return decode(code, s)


def weight_sums(width, cs_refs, xs_refs, f_ref):
    pieces, rows, padded = f_ref.shape
    ch = xs_refs[0].shape[0] // pieces
    for p in range(pieces):
        f_ref[p, :, width:] = jnp.zeros((rows, padded - width), F32)
    got = lax.dot_general(cs_refs[0][...], xs_refs[0][...], NT, preferred_element_type=F32)
    got = got + lax.dot_general(cs_refs[1][...], xs_refs[1][...], NT, preferred_element_type=F32)
    for t in range(TAPS):
        for p in range(pieces):
            f_ref[p, :, t * ch : (t + 1) * ch] = got[t * rows : (t + 1) * rows, p * ch : (p + 1) * ch]


def shifted_rows(far, cot_ref, cs_ref):
    nf, ch, cells = cot_ref.shape
    rows = cs_ref.shape[0] // TAPS
    block = rows // 2
    me = lax.axis_index("dp")
    z, core = me // 2, me % 2
    a = lax.broadcasted_iota(jnp.int32, (rows, ch), 0)
    o = lax.broadcasted_iota(jnp.int32, (rows, ch), 1)
    near = z ^ 1 if far else z
    layer = jnp.where(a < block, near, near ^ 2)
    want = (2 * layer + core) * block + jnp.where(a < block, a, a - block)
    pick = (o == want).astype(F32).astype(BF16)
    for f in range(nf):
        chosen = jnp.dot(pick, cot_ref[f], preferred_element_type=F32)
        at = f * cells
        for t, tap in all_moved(chosen):
            cs_ref[t * rows : (t + 1) * rows, at : at + cells] = tap.astype(BF16)


def frames_in_a_row(x_ref, xs_ref):
    nf, _, cells = x_ref.shape
    for f in range(nf):
        xs_ref[:, f * cells : (f + 1) * cells] = x_ref[f]


def own_rows_kernel(cot_ref, x_ref, cs_ref, xs_ref):
    shifted_rows(True, cot_ref, cs_ref)
    frames_in_a_row(x_ref, xs_ref)


def first_send_kernel(width, cs_ref, xs_ref, cot2_ref, x2_ref, x_ref, send_ref, cs2_ref, xs2_ref, copy_ref, f_ref):
    shifted_rows(True, cot2_ref, cs2_ref)
    frames_in_a_row(x2_ref, xs2_ref)
    copy_ref[...] = x_ref[...]
    weight_sums(width, (cs_ref, cs2_ref), (xs_ref, xs2_ref), f_ref)
    put_rows_coded(send_ref, (0,), f_ref[0], width)


def first_keep_kernel(width, cot_ref, cot2_ref, xs_ref, xs2_ref, w_hbm, keep_ref, cs_ref, cs2_ref, w_ref, sem):
    copies = load_taps(w_hbm, w_ref, sem, xs_ref.shape[0], w_ref.shape[1])
    shifted_rows(False, cot_ref, cs_ref)
    shifted_rows(False, cot2_ref, cs2_ref)
    weight_sums(width, (cs_ref, cs2_ref), (xs_ref, xs2_ref), keep_ref)
    for c in copies:
        c.wait()


def later_send_kernel(width, cs_ref, cs2_ref, xs_ref, xs2_ref, send_ref, f_ref):
    weight_sums(width, (cs_ref, cs2_ref), (xs_ref, xs2_ref), f_ref)
    put_rows_coded(send_ref, (0,), f_ref[0], width)


def later_keep_kernel(width, cs_ref, cs2_ref, *refs):
    if len(refs) == 3:
        xs_ref, xs2_ref, keep_ref = refs
        weight_sums(width, (cs_ref, cs2_ref), (xs_ref, xs2_ref), keep_ref)
    else:
        x0, x02, x1, x12, keep0_ref, keep1_ref, xs_ref, xs2_ref, f_ref = refs
        ch = x0.shape[0]
        xs_ref[:ch] = x0[...]
        xs_ref[ch:] = x1[...]
        xs2_ref[:ch] = x02[...]
        xs2_ref[ch:] = x12[...]
        weight_sums(width, (cs_ref, cs2_ref), (xs_ref, xs2_ref), f_ref)
        keep0_ref[0] = f_ref[0]
        keep1_ref[0] = f_ref[1]


def second_weight_kernel(width, pieces, *refs):
    ins, send_ref, keep_refs = refs[: 2 * pieces], refs[2 * pieces], refs[2 * pieces + 1 :]
    parts = []
    for p in range(pieces):
        keep_ref, recv_ref = ins[2 * p : 2 * p + 2]
        _, rows, padded = keep_ref.shape
        half = rows // 2
        total = keep_ref[0] + take_rows_coded(recv_ref[0], width)
        keep_refs[p][...] = total[:half]
        lane = lax.broadcasted_iota(jnp.int32, (half, padded), 1)
        far = jnp.where(lane < width, total[half:], 0.0)
        s = scale_of(jnp.max(jnp.abs(far), axis=1, keepdims=True))
        parts.append(jnp.where(lane < width, encode(far, s), s))
    if pieces == 1:
        left = send_ref.shape[1]
        fill = jnp.broadcast_to(s, (half, 2 * left - padded))
        parts = [parts[0][:, :left], jnp.concatenate([parts[0][:, left:], fill], axis=1)]
    send_ref[...] = jnp.concatenate(parts, axis=0).astype(BF16)


def unstacked(ref, padded):
    code = ref[...].astype(F32)
    half, left = code.shape[0] // 2, code.shape[1]
    return jnp.concatenate([code[:half], code[half:, : padded - left]], axis=1)


def finish_weight_kernel(width, keep_ref, recv_ref, out_ref):
    out_ref[...] = keep_ref[...] + take_rows_coded(unstacked(recv_ref, keep_ref.shape[1]), width)


def last_weight_kernel(width, side, *refs):
    out_hbm, acc, stage, sem = refs[-4:]
    blk = lax.axis_index("blk")
    ch = width // TAPS
    first = blk % 2
    acc[first] = refs[0][...]
    if side == 0:
        acc[1 - first] = refs[1][...]
    else:
        acc[1 - first] = refs[1][...] + take_rows_coded(unstacked(refs[2], refs[1].shape[1]), width)
    start = pl.multiple_of((blk ^ side) // 2 * (2 * ch), 128)
    copies = []
    for t in range(TAPS):
        for q in range(2):
            stage[t, :, q * ch : (q + 1) * ch] = acc[q, :, t * ch : (t + 1) * ch]
        copies.append(
            pltpu.make_async_copy(
                stage.at[t], out_hbm.at[:, pl.ds(pl.multiple_of(t * 4 * ch + start, 128), 2 * ch)], sem.at[t]
            )
        )
        copies[-1].start()
    for c in copies:
        c.wait()


def put_columns_coded(send_ref, lead, left, right):
    ch, cells = left.shape
    scales = []
    for k, v in enumerate((left, right)):
        s = scale_of(jnp.max(jnp.abs(v), axis=0, keepdims=True))
        send_ref[lead + (slice(k * ch, (k + 1) * ch),)] = encode(v, s).astype(BF16)
        scales.append(jnp.broadcast_to(s, (8, cells)))
    send_ref[lead + (slice(2 * ch, 2 * ch + 16),)] = jnp.concatenate(scales, axis=0).astype(BF16)


def take_columns_coded(ref, lead, ch):
    scales = ref[lead + (slice(2 * ch, 2 * ch + 16),)].astype(F32)
    return [
        decode(ref[lead + (slice(k * ch, (k + 1) * ch),)], scales[8 * k : 8 * k + 1]) for k in range(2)
    ]


def load_taps(w_hbm, w_ref, sem, rows, all_ch):
    copies = [
        pltpu.make_async_copy(
            w_hbm.at[:, pl.ds(t * all_ch, all_ch)], w_ref.at[pl.ds(t * rows, rows)], sem.at[t]
        )
        for t in range(TAPS)
    ]
    for c in copies:
        c.start()
    return copies


def frame_grad_kernel(mask, f0, w_ref, cot_hbm, send_ref, keep_ref, cot_ref, cs_ref, out_ref, sem):
    _, ch, cells = cot_hbm.shape
    all_ch = w_ref.shape[1]
    load = pltpu.make_async_copy(cot_hbm.at[pl.ds(f0, 2)], cot_ref, sem)
    load.start()
    load.wait()
    for f in range(2):
        for t, tap in all_moved(cot_ref[f].astype(F32)):
            cs_ref[t * ch : (t + 1) * ch, f * cells : (f + 1) * cells] = tap.astype(BF16)
    tile = 256
    for i0 in range(0, all_ch, tile):
        out_ref[i0 : i0 + tile, :] = lax.dot_general(
            w_ref[:, i0 : i0 + tile], cs_ref[...], TN, preferred_element_type=F32
        )
    blk = lax.axis_index("blk")

    def block(q, f):
        return out_ref[pl.ds(pl.multiple_of(q * ch, 16), ch), f * cells : (f + 1) * cells]

    for k, q in enumerate((blk ^ mask, blk ^ 3)):
        put_columns_coded(send_ref, (k,), block(q, 0), block(q, 1))
    for k, q in enumerate((blk, blk ^ (3 - mask))):
        for f in range(2):
            keep_ref[k, f * ch : (f + 1) * ch, :] = block(q, f)


def second_frame_kernel(k, r, s, k2):
    ch = k.shape[1] // 2
    for b in range(2):
        got = take_columns_coded(r, (b,), ch)
        sums = [k[b, f * ch : (f + 1) * ch, :] + got[f] for f in range(2)]
        if b == 0:
            for f in range(2):
                k2[f * ch : (f + 1) * ch, :] = sums[f]
        else:
            put_columns_coded(s, (), sums[0], sums[1])


def last_frame_kernel(f0, k, r, *refs):
    out_hbm, stage, sem = refs[-3:]
    ch = stage.shape[1]
    got = take_columns_coded(r, (), ch)
    for f in range(2):
        stage[f] = (k[f * ch : (f + 1) * ch, :] + got[f]).astype(BF16)
    copy = pltpu.make_async_copy(stage, out_hbm.at[pl.ds(f0, 2)], sem)
    copy.start()
    copy.wait()


def response_kernel(w_ref, bias_ref, x0, x1, x2, x3, out_ref, x_ref, y_ref):
    nf, ch, cells = x0.shape
    blk = lax.axis_index("blk")
    base = jnp.transpose(jnp.broadcast_to(bias_ref[...][None, :], (cells, ch)), (1, 0))

    @pl.loop(0, nf)
    def _(f):
        for jj, x in enumerate((x0, x1, x2, x3)):
            x_ref[pl.ds(pl.multiple_of((blk ^ jj) * ch, 16), ch), :] = x[f]
        y_ref[...] = jnp.dot(w_ref[...], x_ref[...], preferred_element_type=F32)
        total = base
        for ky in range(3):
            line = None
            for kx in range(3):
                t = 3 * ky + kx
                part = col_moved(y_ref[t * ch : (t + 1) * ch, :], 1 - kx)
                line = part if line is None else line + part
            total = total + row_moved(line, 1 - ky)
        out_ref[f] = total.astype(BF16)


def params(mib):
    return pltpu.CompilerParams(vmem_limit_bytes=mib * 2**20)


def shape(dims, dtype):
    return jax.ShapeDtypeStruct(dims, dtype)


def swap_core(x):
    return lax.ppermute(x, "dp", [(d, d ^ 1) for d in range(8)])


def swap_layer(x, mask):
    return lax.ppermute(x, "dp", [(d, d ^ (2 * mask)) for d in range(8)])


def swap_block(x, mask):
    return lax.ppermute(x, "blk", [(d, d ^ mask) for d in range(4)])


def run(kernel, name, key, after, args, in_specs, out_shape, out_specs, scratch=(), **more):
    outs = out_shape if isinstance(out_shape, tuple) else (out_shape,)
    specs = out_specs if isinstance(out_specs, tuple) else (out_specs,)
    waits = [] if after is None else [after]
    n = len(waits)
    mark = pl.BlockSpec((8, 128), lambda *_: (0, 0))

    def body(*refs):
        ins = n + len(args)
        refs[ins + len(outs)][...] = jnp.zeros((8, 128), F32)
        kernel(*refs[n : ins + len(outs)], *refs[ins + len(outs) + 1 :])

    *got, token = pl.pallas_call(
        body,
        out_shape=(*outs, shape((8, 128), F32)),
        in_specs=[mark] * n + list(in_specs),
        out_specs=(*specs, mark),
        scratch_shapes=list(scratch),
        compiler_params=params(ROOM[key]),
        cost_estimate=pl.CostEstimate(flops=int(COST[key] * RATE), bytes_accessed=1024, transcendentals=0),
        name=name,
        **more,
    )(*waits, *args)
    return (*got, token)


def small_body(frames, weight, bias, cotangent):
    nf, ch, cells = frames.shape
    all_ch = 4 * ch
    rows = ch // 2
    half, quarter = rows // 2, rows // 4
    width = TAPS * ch
    padded = -(-(width + 1) // 128) * 128
    left = -(-(padded // 2) // 128) * 128

    sums = shape((1, half, padded), F32)
    code = shape((1, half, padded), BF16)
    row_cs = shape((TAPS * half, nf * cells), BF16)
    row_xs = shape((ch, nf * cells), BF16)
    kept = shape((quarter, padded), F32)

    def simple(kernel, name, key, after, args, outs, scratch=()):
        return run(kernel, name, key, after, args, [VMEM] * len(args), outs, (VMEM,) * len(outs), scratch)

    def later_keep(key, after, *args):
        n = (len(args) - 2) // 2
        scratch = [pltpu.VMEM((2 * ch, nf * cells), BF16)] * 2 + [pltpu.VMEM((2, half, padded), F32)]
        return simple(
            functools.partial(later_keep_kernel, width),
            "weight_keep",
            key,
            after,
            args,
            (sums,) * n,
            scratch if n == 2 else (),
        )

    def second(key, after, *args):
        n = len(args) // 2
        out = (2 * quarter, padded) if n == 2 else (2 * quarter, left)
        return simple(
            functools.partial(second_weight_kernel, width, n),
            "weight_second",
            key,
            after,
            args,
            (shape(out, BF16),) + (kept,) * n,
        )

    def frame_part(key, after, mask, f0):
        return run(
            functools.partial(frame_grad_kernel, mask, f0),
            "frame_part",
            key,
            after,
            (taps, cotangent),
            [VMEM, HBM],
            (shape((2, 2 * ch + 16, cells), BF16), shape((2, 2 * ch, cells), F32)),
            (VMEM, VMEM),
            [
                pltpu.VMEM((2, ch, cells), BF16),
                pltpu.VMEM((TAPS * ch, 2 * cells), BF16),
                pltpu.VMEM((all_ch, 2 * cells), F32),
                pltpu.SemaphoreType.DMA,
            ],
        )

    def second_frame(key, after, *args):
        outs = (shape((2 * ch + 16, cells), BF16), shape((2 * ch, cells), F32))
        return simple(second_frame_kernel, "frame_second", key, after, args, outs)

    def last_frame(key, after, f0, parts, held):
        more = {} if held is None else {"input_output_aliases": {3: 0}}
        return run(
            functools.partial(last_frame_kernel, f0),
            "frame_last",
            key,
            after,
            parts if held is None else (*parts, held),
            [VMEM] * 2 + ([] if held is None else [HBM]),
            shape((nf, ch, cells), BF16),
            HBM,
            [pltpu.VMEM((2, ch, cells), BF16), pltpu.SemaphoreType.DMA],
            **more,
        )

    def respond(key, after, *xs):
        return run(
            response_kernel,
            "response",
            key,
            after,
            (taps, bias, *xs),
            [VMEM] * 6,
            shape((nf, ch, cells), BF16),
            VMEM,
            [pltpu.VMEM((all_ch, cells), BF16), pltpu.VMEM((TAPS * ch, cells), F32)],
        )

    def last_weight(key, after, side, parts, held):
        more = {} if held is None else {"input_output_aliases": {len(parts) + 1: 0}}
        return run(
            functools.partial(last_weight_kernel, width, side),
            "weight_last",
            key,
            after,
            parts if held is None else (*parts, held),
            [VMEM] * len(parts) + ([] if held is None else [HBM]),
            shape((quarter, TAPS * all_ch), F32),
            HBM,
            [
                pltpu.VMEM((2, quarter, padded), F32),
                pltpu.VMEM((TAPS, quarter, 2 * ch), F32),
                pltpu.SemaphoreType.DMA((TAPS,)),
            ],
            **more,
        )

    cot2 = swap_core(cotangent)
    own2 = swap_core(frames)
    near = {"x": swap_block(frames, 1)}

    t = None
    send, keep, recv, xs, cs = {}, {}, {}, {}, {}
    fsend, fkeep, frecv = {}, {}, {}
    for step in ORDER:
        if step == "pre":
            cs_own, xs_own, t = simple(own_rows_kernel, "own_rows", step, t, (cotangent, frames), (row_cs, row_xs))
        elif step == "a":
            send["a"], cs2, xs2, again, t = simple(
                functools.partial(first_send_kernel, width),
                "weight_send",
                step,
                t,
                (cs_own, xs_own, cot2, own2, frames),
                (code, row_cs, row_xs, shape((nf, ch, cells), BF16)),
                [pltpu.VMEM((1, half, padded), F32)],
            )
            cs["far"], xs["a"] = (cs_own, cs2), (xs_own, xs2)
            recv["a"] = swap_layer(send["a"], 1)
            near["y"] = swap_block(frames, 2)
        elif step in ("gx", "gy", "gd"):
            k = step[1]
            row, t = simple(frames_in_a_row, "rows", step, t, (near[k],), (row_xs,))
            xs["bcd"["xyd".index(k)]] = (row, swap_core(row))
            if k == "x":
                near["d"] = swap_block(near["x"], 2)
        elif step in ("b", "c", "d"):
            send[step], t = simple(
                functools.partial(later_send_kernel, width),
                "weight_send",
                step,
                t,
                (*cs["far"], *xs[step]),
                (code,),
                [pltpu.VMEM((1, half, padded), F32)],
            )
            recv[step] = swap_layer(send[step], 1)
        elif step == "ka":
            keep["a"], cs_near, cs2_near, taps, t = run(
                functools.partial(first_keep_kernel, width),
                "weight_keep",
                step,
                t,
                (cotangent, cot2, *xs["a"], weight),
                [VMEM] * 4 + [ANY],
                (sums, row_cs, row_cs, shape((TAPS * ch, all_ch), BF16)),
                (VMEM,) * 4,
                [pltpu.SemaphoreType.DMA((TAPS,))],
            )
            cs["near"] = (cs_near, cs2_near)
        elif step == "kb":
            keep["b"], keep["c"], t = later_keep(step, t, *cs["near"], *xs["b"], *xs["c"])
        elif step == "kd":
            keep["d"], t = later_keep(step, t, *cs["near"], *xs["d"])
        elif step in ("a2", "b2", "c2", "d2"):
            k = step[0]
            send[step], keep[step], t = second(step, t, keep[k], recv[k])
            recv[step] = swap_layer(send[step], 2)
        elif step in ("fx", "fy"):
            k = 1 if step == "fx" else 2
            fsend[k], fkeep[k], t = frame_part(step, t, k, 2 * k - 2)
            frecv[k] = swap_block(fsend[k], k)
        elif step in ("f2x", "f2y"):
            k = 1 if step == "f2x" else 2
            fsend[k + 2], fkeep[k + 2], t = second_frame(step, t, fkeep[k], frecv[k])
            frecv[k + 2] = swap_block(fsend[k + 2], 3 - k)
        elif step == "flx":
            fheld, t = last_frame(step, t, 0, (fkeep[3], frecv[3]), None)
        elif step == "fly":
            frame_grad, t = last_frame(step, t, 2, (fkeep[4], frecv[4]), fheld)
        elif step == "resp":
            response, t = respond(step, t, again, near["x"], near["y"], near["d"])
        elif step in ("ea", "eb", "ec"):
            k = step[1] + "2"
            keep[step], t = simple(
                functools.partial(finish_weight_kernel, width), "weight_end", step, t, (keep[k], recv[k]), (kept,)
            )
        elif step == "wab":
            held, t = last_weight(step, t, 0, (keep["ea"], keep["eb"]), None)
        else:
            weight_grad, t = last_weight(step, t, 2, (keep["ec"], keep["d2"], recv["d2"]), held)
    return (response, frame_grad, weight_grad)


def solution(mesh):
    small = mesh.shape["dp"] == 8 and mesh.shape["blk"] == 4
    return jax.shard_map(
        small_body if small else general_body,
        mesh=mesh,
        in_specs=(P("dp", "blk", None), P("blk", None), P("blk"), P("dp", "blk", None)),
        out_specs=(P("dp", "blk", None), P("dp", "blk", None), P(("blk", "dp"), None)),
        check_vma=False,
    )
```

```python
import functools

import jax
import jax.numpy as jnp
from jax import lax
from jax.experimental import pallas as pl
from jax.experimental.pallas import tpu as pltpu
from jax.sharding import PartitionSpec as P

WD = 16
TAPS = 9
F32, BF16 = jnp.float32, jnp.bfloat16
NT = (((1,), (1,)), ((), ()))
TN = (((0,), (0,)), ((), ()))
VMEM = pl.BlockSpec(memory_space=pltpu.VMEM)
ANY = pl.BlockSpec(memory_space=pl.ANY)
HBM = pl.BlockSpec(memory_space=pltpu.HBM)
SPAN = 125.0
RATE = 5e8
ROOM = dict(pre=61, a=12, fx=18, gx=4, gy=4, gd=4, ka=20, a2=8, b=10, fy=18, c=10, kb=18, f2x=8, b2=8, kd=10, c2=8, d=10, f2y=8, wab=10, flx=6, d2=8, resp=18, fly=6, wcd=10, ea=8, eb=8, ec=8)
ORDER = ("pre", "a", "ka", "fx", "gx", "gy", "a2", "b", "c", "kb", "f2x", "ea", "gd", "fy", "b2", "d", "kd", "c2", "eb", "f2y", "wab", "flx", "d2", "resp", "fly", "ec", "wcd")
COST = dict(pre=20, a=45, ka=40, fx=85, gx=10, gy=10, gd=10, b=40, c=40, d=40, kb=50, kd=40, fy=85, a2=7, b2=7, c2=7, resp=110, f2x=12, f2y=12, d2=7, flx=10, fly=10, wab=24, wcd=24, ea=7, eb=7, ec=7)


def shift_cells(maps, step_row, step_col):
    cells = maps.shape[-1]
    margin = WD + 1
    widths = [(0, 0)] * (maps.ndim - 1) + [(margin, margin)]
    flat = jnp.pad(maps, widths)
    begin = margin + step_row * WD + step_col
    moved = lax.slice_in_dim(flat, begin, begin + cells, axis=maps.ndim - 1)
    column = jnp.arange(cells, dtype=jnp.int32) % WD + step_col
    keeper = ((column >= 0) & (column < WD)).astype(maps.dtype)
    return moved * keeper


def general_body(frames, weight, bias, cotangent):
    nframe = frames.shape[0]
    local_ch = frames.shape[1]
    cells = frames.shape[2]
    whole = lax.all_gather(frames, "blk", axis=1, tiled=True)
    all_ch = whole.shape[1]
    total = jnp.zeros((nframe, local_ch, cells), F32)
    grads = []
    for tap in range(TAPS):
        ky, kx = divmod(tap, 3)
        piece = shift_cells(whole, ky - 1, kx - 1)
        w_tap = weight[:, tap * all_ch : (tap + 1) * all_ch]
        total = total + jnp.einsum("oi,fic->foc", w_tap, piece, preferred_element_type=F32)
        grads.append(
            lax.dot_general(cotangent, piece, (((0, 2), (0, 2)), ((), ())), preferred_element_type=F32)
        )
    response = (total + bias[None, :, None]).astype(BF16)
    local_grad = jnp.concatenate(grads, axis=1)
    weight_grad = lax.psum_scatter(local_grad, "dp", scatter_dimension=0, tiled=True)
    cot_moved = [shift_cells(cotangent, 1 - tap // 3, 1 - tap % 3) for tap in range(TAPS)]
    accum = jnp.zeros((all_ch, nframe, cells), F32)
    for tap in range(TAPS):
        w_cols = lax.slice_in_dim(weight, tap * all_ch, (tap + 1) * all_ch, axis=1)
        accum = accum + jnp.einsum("oi,foc->ifc", w_cols, cot_moved[tap], preferred_element_type=F32)
    shares = lax.psum_scatter(accum, "blk", scatter_dimension=0, tiled=True)
    frame_grad = jnp.transpose(shares, (1, 0, 2)).astype(BF16)
    return (response, frame_grad, weight_grad)


def scale_of(largest):
    return (jnp.maximum(largest, 1e-30) * 1.01).astype(BF16).astype(F32)


def encode(x, s):
    y = jnp.exp2(jnp.abs(x) * (2 * SPAN / s) - SPAN)
    return jnp.where(x < 0, -y, y)


def decode(code, s):
    y = code.astype(F32)
    v = (jnp.log2(jnp.abs(y)) + SPAN) * (s * (0.5 / SPAN))
    return jnp.where(y < 0, -v, v)


LANES = 128


def col_moved(x, dx):
    if dx == 0:
        return x
    rows, cells = x.shape
    col = lax.broadcasted_iota(jnp.int32, (rows, LANES), 1) % WD
    ok = (col >= dx) if dx > 0 else (col < WD + dx)
    parts = [
        jnp.where(ok, pltpu.roll(x[:, at : at + LANES], dx % LANES, 1), 0.0) for at in range(0, cells, LANES)
    ]
    return jnp.concatenate(parts, axis=1)


def row_moved(x, dy):
    if dy == 0:
        return x
    rows, cells = x.shape
    by = dy * WD
    lane = lax.broadcasted_iota(jnp.int32, (rows, LANES), 1)
    parts = [pltpu.roll(x[:, at : at + LANES], by % LANES, 1) for at in range(0, cells, LANES)]
    if dy > 0:
        parts = [jnp.where(lane < by, parts[k - 1] if k else 0.0, parts[k]) for k in range(len(parts))]
    else:
        after = parts[1:] + [0.0]
        parts = [jnp.where(lane >= LANES + by, after[k], parts[k]) for k in range(len(parts))]
    return jnp.concatenate(parts, axis=1)


def all_moved(x):
    for kx in range(3):
        along = col_moved(x, kx - 1)
        for ky in range(3):
            yield 3 * ky + kx, row_moved(along, ky - 1)


def put_rows_coded(out_ref, lead, values, width):
    rows, padded = values.shape
    s = scale_of(jnp.max(jnp.abs(values), axis=1, keepdims=True))
    codes = encode(values, s)
    last = padded - 128
    lane = lax.broadcasted_iota(jnp.int32, (rows, 128), 1) + last
    out_ref[lead + (slice(None), slice(0, last))] = codes[:, :last].astype(BF16)
    tail = jnp.where(lane < width, codes[:, last:], s)
    out_ref[lead + (slice(None), slice(last, padded))] = tail.astype(BF16)


def take_rows_coded(code, width):
    s = code[:, width : width + 1].astype(F32)
    return decode(code, s)


def weight_sums(width, cs_refs, xs_refs, f_ref):
    pieces, rows, padded = f_ref.shape
    ch = xs_refs[0].shape[0] // pieces
    for p in range(pieces):
        f_ref[p, :, width:] = jnp.zeros((rows, padded - width), F32)
    got = lax.dot_general(cs_refs[0][...], xs_refs[0][...], NT, preferred_element_type=F32)
    got = got + lax.dot_general(cs_refs[1][...], xs_refs[1][...], NT, preferred_element_type=F32)
    for t in range(TAPS):
        for p in range(pieces):
            f_ref[p, :, t * ch : (t + 1) * ch] = got[t * rows : (t + 1) * rows, p * ch : (p + 1) * ch]


def shifted_rows(far, cot_ref, cs_ref):
    nf, ch, cells = cot_ref.shape
    rows = cs_ref.shape[0] // TAPS
    block = rows // 2
    me = lax.axis_index("dp")
    z, core = me // 2, me % 2
    a = lax.broadcasted_iota(jnp.int32, (rows, ch), 0)
    o = lax.broadcasted_iota(jnp.int32, (rows, ch), 1)
    near = z ^ 1 if far else z
    layer = jnp.where(a < block, near, near ^ 2)
    want = (2 * layer + core) * block + jnp.where(a < block, a, a - block)
    pick = (o == want).astype(F32).astype(BF16)
    for f in range(nf):
        chosen = jnp.dot(pick, cot_ref[f], preferred_element_type=F32)
        at = f * cells
        for t, tap in all_moved(chosen):
            cs_ref[t * rows : (t + 1) * rows, at : at + cells] = tap.astype(BF16)


def frames_in_a_row(x_ref, xs_ref):
    nf, _, cells = x_ref.shape
    for f in range(nf):
        xs_ref[:, f * cells : (f + 1) * cells] = x_ref[f]


def own_rows_kernel(cot_ref, x_ref, cs_ref, xs_ref):
    shifted_rows(True, cot_ref, cs_ref)
    frames_in_a_row(x_ref, xs_ref)


def first_send_kernel(width, cs_ref, xs_ref, cot2_ref, x2_ref, send_ref, cs2_ref, xs2_ref, f_ref):
    shifted_rows(True, cot2_ref, cs2_ref)
    frames_in_a_row(x2_ref, xs2_ref)
    weight_sums(width, (cs_ref, cs2_ref), (xs_ref, xs2_ref), f_ref)
    put_rows_coded(send_ref, (0,), f_ref[0], width)


def first_keep_kernel(width, cot_ref, cot2_ref, xs_ref, xs2_ref, w_hbm, keep_ref, cs_ref, cs2_ref, w_ref, sem):
    copies = load_taps(w_hbm, w_ref, sem, xs_ref.shape[0], w_ref.shape[1])
    shifted_rows(False, cot_ref, cs_ref)
    shifted_rows(False, cot2_ref, cs2_ref)
    weight_sums(width, (cs_ref, cs2_ref), (xs_ref, xs2_ref), keep_ref)
    for c in copies:
        c.wait()


def later_send_kernel(width, cs_ref, cs2_ref, xs_ref, xs2_ref, send_ref, f_ref):
    weight_sums(width, (cs_ref, cs2_ref), (xs_ref, xs2_ref), f_ref)
    put_rows_coded(send_ref, (0,), f_ref[0], width)


def later_keep_kernel(width, cs_ref, cs2_ref, *refs):
    if len(refs) == 3:
        xs_ref, xs2_ref, keep_ref = refs
        weight_sums(width, (cs_ref, cs2_ref), (xs_ref, xs2_ref), keep_ref)
    else:
        x0, x02, x1, x12, keep0_ref, keep1_ref, xs_ref, xs2_ref, f_ref = refs
        ch = x0.shape[0]
        xs_ref[:ch] = x0[...]
        xs_ref[ch:] = x1[...]
        xs2_ref[:ch] = x02[...]
        xs2_ref[ch:] = x12[...]
        weight_sums(width, (cs_ref, cs2_ref), (xs_ref, xs2_ref), f_ref)
        keep0_ref[0] = f_ref[0]
        keep1_ref[0] = f_ref[1]


def second_weight_kernel(width, pieces, *refs):
    ins, send_ref, keep_refs = refs[: 2 * pieces], refs[2 * pieces], refs[2 * pieces + 1 :]
    parts = []
    for p in range(pieces):
        keep_ref, recv_ref = ins[2 * p : 2 * p + 2]
        _, rows, padded = keep_ref.shape
        half = rows // 2
        total = keep_ref[0] + take_rows_coded(recv_ref[0], width)
        keep_refs[p][...] = total[:half]
        lane = lax.broadcasted_iota(jnp.int32, (half, padded), 1)
        far = jnp.where(lane < width, total[half:], 0.0)
        s = scale_of(jnp.max(jnp.abs(far), axis=1, keepdims=True))
        parts.append(jnp.where(lane < width, encode(far, s), s))
    if pieces == 1:
        left = send_ref.shape[1]
        fill = jnp.broadcast_to(s, (half, 2 * left - padded))
        parts = [parts[0][:, :left], jnp.concatenate([parts[0][:, left:], fill], axis=1)]
    send_ref[...] = jnp.concatenate(parts, axis=0).astype(BF16)


def unstacked(ref, padded):
    code = ref[...].astype(F32)
    half, left = code.shape[0] // 2, code.shape[1]
    return jnp.concatenate([code[:half], code[half:, : padded - left]], axis=1)


def finish_weight_kernel(width, keep_ref, recv_ref, out_ref):
    out_ref[...] = keep_ref[...] + take_rows_coded(unstacked(recv_ref, keep_ref.shape[1]), width)


def last_weight_kernel(width, side, *refs):
    out_hbm, acc, stage, sem = refs[-4:]
    blk = lax.axis_index("blk")
    ch = width // TAPS
    first = blk % 2
    acc[first] = refs[0][...]
    if side == 0:
        acc[1 - first] = refs[1][...]
    else:
        acc[1 - first] = refs[1][...] + take_rows_coded(unstacked(refs[2], refs[1].shape[1]), width)
    start = pl.multiple_of((blk ^ side) // 2 * (2 * ch), 128)
    copies = []
    for t in range(TAPS):
        for q in range(2):
            stage[t, :, q * ch : (q + 1) * ch] = acc[q, :, t * ch : (t + 1) * ch]
        copies.append(
            pltpu.make_async_copy(
                stage.at[t], out_hbm.at[:, pl.ds(pl.multiple_of(t * 4 * ch + start, 128), 2 * ch)], sem.at[t]
            )
        )
        copies[-1].start()
    for c in copies:
        c.wait()


def put_columns_coded(send_ref, lead, left, right):
    ch, cells = left.shape
    scales = []
    for k, v in enumerate((left, right)):
        s = scale_of(jnp.max(jnp.abs(v), axis=0, keepdims=True))
        send_ref[lead + (slice(k * ch, (k + 1) * ch),)] = encode(v, s).astype(BF16)
        scales.append(jnp.broadcast_to(s, (8, cells)))
    send_ref[lead + (slice(2 * ch, 2 * ch + 16),)] = jnp.concatenate(scales, axis=0).astype(BF16)


def take_columns_coded(ref, lead, ch):
    scales = ref[lead + (slice(2 * ch, 2 * ch + 16),)].astype(F32)
    return [
        decode(ref[lead + (slice(k * ch, (k + 1) * ch),)], scales[8 * k : 8 * k + 1]) for k in range(2)
    ]


def load_taps(w_hbm, w_ref, sem, rows, all_ch):
    copies = [
        pltpu.make_async_copy(
            w_hbm.at[:, pl.ds(t * all_ch, all_ch)], w_ref.at[pl.ds(t * rows, rows)], sem.at[t]
        )
        for t in range(TAPS)
    ]
    for c in copies:
        c.start()
    return copies


def frame_grad_kernel(mask, f0, w_ref, cot_hbm, send_ref, keep_ref, cot_ref, cs_ref, out_ref, sem):
    _, ch, cells = cot_hbm.shape
    all_ch = w_ref.shape[1]
    load = pltpu.make_async_copy(cot_hbm.at[pl.ds(f0, 2)], cot_ref, sem)
    load.start()
    load.wait()
    for f in range(2):
        for t, tap in all_moved(cot_ref[f].astype(F32)):
            cs_ref[t * ch : (t + 1) * ch, f * cells : (f + 1) * cells] = tap.astype(BF16)
    tile = 256
    for i0 in range(0, all_ch, tile):
        out_ref[i0 : i0 + tile, :] = lax.dot_general(
            w_ref[:, i0 : i0 + tile], cs_ref[...], TN, preferred_element_type=F32
        )
    blk = lax.axis_index("blk")

    def block(q, f):
        return out_ref[pl.ds(pl.multiple_of(q * ch, 16), ch), f * cells : (f + 1) * cells]

    for k, q in enumerate((blk ^ mask, blk ^ 3)):
        put_columns_coded(send_ref, (k,), block(q, 0), block(q, 1))
    for k, q in enumerate((blk, blk ^ (3 - mask))):
        for f in range(2):
            keep_ref[k, f * ch : (f + 1) * ch, :] = block(q, f)


def second_frame_kernel(k, r, s, k2):
    ch = k.shape[1] // 2
    for b in range(2):
        got = take_columns_coded(r, (b,), ch)
        sums = [k[b, f * ch : (f + 1) * ch, :] + got[f] for f in range(2)]
        if b == 0:
            for f in range(2):
                k2[f * ch : (f + 1) * ch, :] = sums[f]
        else:
            put_columns_coded(s, (), sums[0], sums[1])


def last_frame_kernel(f0, k, r, *refs):
    out_hbm, stage, sem = refs[-3:]
    ch = stage.shape[1]
    got = take_columns_coded(r, (), ch)
    for f in range(2):
        stage[f] = (k[f * ch : (f + 1) * ch, :] + got[f]).astype(BF16)
    copy = pltpu.make_async_copy(stage, out_hbm.at[pl.ds(f0, 2)], sem)
    copy.start()
    copy.wait()


def response_kernel(w_ref, bias_ref, x0, x1, x2, x3, out_ref, x_ref, y_ref):
    nf, ch, cells = x0.shape
    blk = lax.axis_index("blk")
    base = jnp.transpose(jnp.broadcast_to(bias_ref[...][None, :], (cells, ch)), (1, 0))

    @pl.loop(0, nf)
    def _(f):
        for jj, x in enumerate((x0, x1, x2, x3)):
            x_ref[pl.ds(pl.multiple_of((blk ^ jj) * ch, 16), ch), :] = x[f]
        y_ref[...] = jnp.dot(w_ref[...], x_ref[...], preferred_element_type=F32)
        total = base
        for ky in range(3):
            line = None
            for kx in range(3):
                t = 3 * ky + kx
                part = col_moved(y_ref[t * ch : (t + 1) * ch, :], 1 - kx)
                line = part if line is None else line + part
            total = total + row_moved(line, 1 - ky)
        out_ref[f] = total.astype(BF16)


def params(mib):
    return pltpu.CompilerParams(vmem_limit_bytes=mib * 2**20)


def shape(dims, dtype):
    return jax.ShapeDtypeStruct(dims, dtype)


def swap_core(x):
    return lax.ppermute(x, "dp", [(d, d ^ 1) for d in range(8)])


def swap_layer(x, mask):
    return lax.ppermute(x, "dp", [(d, d ^ (2 * mask)) for d in range(8)])


def swap_block(x, mask):
    return lax.ppermute(x, "blk", [(d, d ^ mask) for d in range(4)])


def run(kernel, name, key, after, args, in_specs, out_shape, out_specs, scratch=(), **more):
    outs = out_shape if isinstance(out_shape, tuple) else (out_shape,)
    specs = out_specs if isinstance(out_specs, tuple) else (out_specs,)
    waits = [] if after is None else [after]
    n = len(waits)
    mark = pl.BlockSpec((8, 128), lambda *_: (0, 0))

    def body(*refs):
        ins = n + len(args)
        refs[ins + len(outs)][...] = jnp.zeros((8, 128), F32)
        kernel(*refs[n : ins + len(outs)], *refs[ins + len(outs) + 1 :])

    *got, token = pl.pallas_call(
        body,
        out_shape=(*outs, shape((8, 128), F32)),
        in_specs=[mark] * n + list(in_specs),
        out_specs=(*specs, mark),
        scratch_shapes=list(scratch),
        compiler_params=params(ROOM[key]),
        cost_estimate=pl.CostEstimate(flops=int(COST[key] * RATE), bytes_accessed=1024, transcendentals=0),
        name=name,
        **more,
    )(*waits, *args)
    return (*got, token)


def small_body(frames, weight, bias, cotangent):
    nf, ch, cells = frames.shape
    all_ch = 4 * ch
    rows = ch // 2
    half, quarter = rows // 2, rows // 4
    width = TAPS * ch
    padded = -(-(width + 1) // 128) * 128
    left = -(-(padded // 2) // 128) * 128

    sums = shape((1, half, padded), F32)
    code = shape((1, half, padded), BF16)
    row_cs = shape((TAPS * half, nf * cells), BF16)
    row_xs = shape((ch, nf * cells), BF16)
    kept = shape((quarter, padded), F32)

    def simple(kernel, name, key, after, args, outs, scratch=()):
        return run(kernel, name, key, after, args, [VMEM] * len(args), outs, (VMEM,) * len(outs), scratch)

    def later_keep(key, after, *args):
        n = (len(args) - 2) // 2
        scratch = [pltpu.VMEM((2 * ch, nf * cells), BF16)] * 2 + [pltpu.VMEM((2, half, padded), F32)]
        return simple(
            functools.partial(later_keep_kernel, width),
            "weight_keep",
            key,
            after,
            args,
            (sums,) * n,
            scratch if n == 2 else (),
        )

    def second(key, after, *args):
        n = len(args) // 2
        out = (2 * quarter, padded) if n == 2 else (2 * quarter, left)
        return simple(
            functools.partial(second_weight_kernel, width, n),
            "weight_second",
            key,
            after,
            args,
            (shape(out, BF16),) + (kept,) * n,
        )

    def frame_part(key, after, mask, f0):
        return run(
            functools.partial(frame_grad_kernel, mask, f0),
            "frame_part",
            key,
            after,
            (taps, cotangent),
            [VMEM, HBM],
            (shape((2, 2 * ch + 16, cells), BF16), shape((2, 2 * ch, cells), F32)),
            (VMEM, VMEM),
            [
                pltpu.VMEM((2, ch, cells), BF16),
                pltpu.VMEM((TAPS * ch, 2 * cells), BF16),
                pltpu.VMEM((all_ch, 2 * cells), F32),
                pltpu.SemaphoreType.DMA,
            ],
        )

    def second_frame(key, after, *args):
        outs = (shape((2 * ch + 16, cells), BF16), shape((2 * ch, cells), F32))
        return simple(second_frame_kernel, "frame_second", key, after, args, outs)

    def last_frame(key, after, f0, parts, held):
        more = {} if held is None else {"input_output_aliases": {3: 0}}
        return run(
            functools.partial(last_frame_kernel, f0),
            "frame_last",
            key,
            after,
            parts if held is None else (*parts, held),
            [VMEM] * 2 + ([] if held is None else [HBM]),
            shape((nf, ch, cells), BF16),
            HBM,
            [pltpu.VMEM((2, ch, cells), BF16), pltpu.SemaphoreType.DMA],
            **more,
        )

    def respond(key, after, *xs):
        return run(
            response_kernel,
            "response",
            key,
            after,
            (taps, bias, *xs),
            [VMEM] * 6,
            shape((nf, ch, cells), BF16),
            VMEM,
            [pltpu.VMEM((all_ch, cells), BF16), pltpu.VMEM((TAPS * ch, cells), F32)],
        )

    def last_weight(key, after, side, parts, held):
        more = {} if held is None else {"input_output_aliases": {len(parts) + 1: 0}}
        return run(
            functools.partial(last_weight_kernel, width, side),
            "weight_last",
            key,
            after,
            parts if held is None else (*parts, held),
            [VMEM] * len(parts) + ([] if held is None else [HBM]),
            shape((quarter, TAPS * all_ch), F32),
            HBM,
            [
                pltpu.VMEM((2, quarter, padded), F32),
                pltpu.VMEM((TAPS, quarter, 2 * ch), F32),
                pltpu.SemaphoreType.DMA((TAPS,)),
            ],
            **more,
        )

    cot2 = swap_core(cotangent)
    own2 = swap_core(frames)
    near = {"x": swap_block(frames, 1), "y": swap_block(frames, 2)}

    t = None
    send, keep, recv, xs, cs = {}, {}, {}, {}, {}
    fsend, fkeep, frecv = {}, {}, {}
    for step in ORDER:
        if step == "pre":
            cs_own, xs_own, t = simple(own_rows_kernel, "own_rows", step, t, (cotangent, frames), (row_cs, row_xs))
        elif step == "a":
            send["a"], cs2, xs2, t = simple(
                functools.partial(first_send_kernel, width),
                "weight_send",
                step,
                t,
                (cs_own, xs_own, cot2, own2),
                (code, row_cs, row_xs),
                [pltpu.VMEM((1, half, padded), F32)],
            )
            cs["far"], xs["a"] = (cs_own, cs2), (xs_own, xs2)
            recv["a"] = swap_layer(send["a"], 1)
        elif step in ("gx", "gy", "gd"):
            k = step[1]
            row, t = simple(frames_in_a_row, "rows", step, t, (near[k],), (row_xs,))
            xs["bcd"["xyd".index(k)]] = (row, swap_core(row))
            if k == "x":
                near["d"] = swap_block(near["x"], 2)
        elif step in ("b", "c", "d"):
            send[step], t = simple(
                functools.partial(later_send_kernel, width),
                "weight_send",
                step,
                t,
                (*cs["far"], *xs[step]),
                (code,),
                [pltpu.VMEM((1, half, padded), F32)],
            )
            recv[step] = swap_layer(send[step], 1)
        elif step == "ka":
            keep["a"], cs_near, cs2_near, taps, t = run(
                functools.partial(first_keep_kernel, width),
                "weight_keep",
                step,
                t,
                (cotangent, cot2, *xs["a"], weight),
                [VMEM] * 4 + [ANY],
                (sums, row_cs, row_cs, shape((TAPS * ch, all_ch), BF16)),
                (VMEM,) * 4,
                [pltpu.SemaphoreType.DMA((TAPS,))],
            )
            cs["near"] = (cs_near, cs2_near)
        elif step == "kb":
            keep["b"], keep["c"], t = later_keep(step, t, *cs["near"], *xs["b"], *xs["c"])
        elif step == "kd":
            keep["d"], t = later_keep(step, t, *cs["near"], *xs["d"])
        elif step in ("a2", "b2", "c2", "d2"):
            k = step[0]
            send[step], keep[step], t = second(step, t, keep[k], recv[k])
            recv[step] = swap_layer(send[step], 2)
        elif step in ("fx", "fy"):
            k = 1 if step == "fx" else 2
            fsend[k], fkeep[k], t = frame_part(step, t, k, 2 * k - 2)
            frecv[k] = swap_block(fsend[k], k)
        elif step in ("f2x", "f2y"):
            k = 1 if step == "f2x" else 2
            fsend[k + 2], fkeep[k + 2], t = second_frame(step, t, fkeep[k], frecv[k])
            frecv[k + 2] = swap_block(fsend[k + 2], 3 - k)
        elif step == "flx":
            fheld, t = last_frame(step, t, 0, (fkeep[3], frecv[3]), None)
        elif step == "fly":
            frame_grad, t = last_frame(step, t, 2, (fkeep[4], frecv[4]), fheld)
        elif step == "resp":
            response, t = respond(step, t, frames, near["x"], near["y"], near["d"])
        elif step in ("ea", "eb", "ec"):
            k = step[1] + "2"
            keep[step], t = simple(
                functools.partial(finish_weight_kernel, width), "weight_end", step, t, (keep[k], recv[k]), (kept,)
            )
        elif step == "wab":
            held, t = last_weight(step, t, 0, (keep["ea"], keep["eb"]), None)
        else:
            weight_grad, t = last_weight(step, t, 2, (keep["ec"], keep["d2"], recv["d2"]), held)
    return (response, frame_grad, weight_grad)


def solution(mesh):
    small = mesh.shape["dp"] == 8 and mesh.shape["blk"] == 4
    return jax.shard_map(
        small_body if small else general_body,
        mesh=mesh,
        in_specs=(P("dp", "blk", None), P("blk", None), P("blk"), P("dp", "blk", None)),
        out_specs=(P("dp", "blk", None), P("dp", "blk", None), P(("blk", "dp"), None)),
        check_vma=False,
    )
```
